32 devices in a mesh: group: 2 (over y), dp: 4 (over z), tensor: 4 (over x, core).
Axes of the slice: x: 2, y: 2, z: 4, core: 2. Of those that a mesh axis runs over, the one named last changes fastest.
Arguments:
- base_heads: bfloat16 [4096, 4096], P(('group', 'dp'), 'tensor'), parts along dimension 0, may hold values from -6 to 6
- source_heads: bfloat16 [4096, 4096], P(('group', 'dp'), 'tensor'), parts along dimension 0, may hold values from -6 to 6
- residual: bfloat16 [4096, 4096], P(('group', 'dp'), 'tensor'), parts along dimension 0, may hold values from -6 to 6
- weight: bfloat16 [4096, 4096], P('tensor', 'dp'), may hold values from -0.09375 to 0.09375
- cotangent: bfloat16 [4096, 4096], P(('group', 'dp')), parts along dimension 0, may hold values from -6 to 6
- send_slots: int32 [8, 4, 128], P(('group', 'dp')), parts along dimension 0, may hold values from -1 to 511, as said below
- recv_slots: int32 [8, 4, 128], P(('group', 'dp')), parts along dimension 0, may hold values from -1 to 511, as said below
- head_mask: int32 [32, 32], P(('group', 'dp'), 'tensor'), parts along dimension 0, may hold values 0 or 1
Outputs:
- layer_out: bfloat16 [4096, 4096], P(('group', 'dp'), 'tensor'), parts along dimension 0
- grad_base: bfloat16 [4096, 4096], P(('group', 'dp'), 'tensor'), parts along dimension 0
- grad_source: bfloat16 [4096, 4096], P(('group', 'dp'), 'tensor'), parts along dimension 0
- grad_weight: float32 [8192, 4096], P(('group', 'tensor'), 'dp'), parts along dimension 0
The draws below stay inside these ranges and needn't reach their ends.
There are 2 independent parts, one for each index of `group`. The reference program is written for one: setup_inputs(seed, part) draws one part's arguments, and reference() takes and returns one part's arrays. A program takes and returns all parts, laid end to end along the dimension named above; an argument that names none is the same for every part. Nothing has to cross between parts.
Inputs may be any that keep to these rules, and one draw needn't show every extreme that they name: send_slots[i, j, k] is a row of dp index i's source tokens sent in slot k to dp index j, or -1 for an empty slot; live slots come first; no source row appears twice; between 1 and 128 slots are live for each i and j, and in every draw one dp index receives 128 rows from every dp index. recv_slots[j, i, k] is the row of dp index j's base tokens that takes the row sent in slot k from dp index i; it is -1 exactly where send_slots[i, j, k] is -1; no base row appears twice.
All inputs are finite; a program needn't handle non-finite values. No bound on the sum of `head_mask` on one device may be relied on, other than what follows from the above.
Results may differ from the reference program's by a relative error of at most 0.009.
Values may be sent and summed in bfloat16 or wider, within the bound.
A program may use at most 128 MiB of HBM per device.

```python
import jax
import jax.numpy as jnp
from jax import lax

D = 4096
HEADS = 32
HDIM = 128
PROMPT = 128
PROMPTS_DEV = 4
HD = 4096
ROWS = 512
TOKENS = 2048
CAP = 128
N_DP = 4
N_TENSOR = 4


def pair_tables(key):
    key = jax.random.fold_in(key, 11)
    key_count, key_full, key_send, key_recv = jax.random.split(key, 4)
    counts = jax.random.randint(key_count, (N_DP, N_DP), 1, CAP + 1)
    full = jax.random.randint(key_full, (), 0, N_DP)
    counts = jnp.where(jnp.arange(N_DP)[None, :] == full, CAP, counts).astype(jnp.int32)
    slot = jnp.arange(CAP, dtype=jnp.int32)
    live = slot[None, None, :] < counts[:, :, None]
    send_off = jnp.cumsum(counts, axis=1) - counts
    recv_off = jnp.cumsum(counts, axis=0) - counts
    send_perm = jax.vmap(lambda k: jax.random.permutation(k, ROWS))(jax.random.split(key_send, N_DP)).astype(jnp.int32)
    recv_perm = jax.vmap(lambda k: jax.random.permutation(k, ROWS))(jax.random.split(key_recv, N_DP)).astype(jnp.int32)
    every = jnp.arange(N_DP, dtype=jnp.int32)
    spos = jnp.minimum(send_off[:, :, None] + slot[None, None, :], ROWS - 1)
    rpos = jnp.minimum(recv_off[:, :, None] + slot[None, None, :], ROWS - 1)
    sent = send_perm[every[:, None, None], spos]
    taken = recv_perm[every[None, :, None], rpos]
    send_table = jnp.where(live, sent, -1).astype(jnp.int32)
    recv_table = jnp.transpose(jnp.where(live, taken, -1), (1, 0, 2)).astype(jnp.int32)
    return (send_table, recv_table)


def draw_send_slots(key, part):
    return pair_tables(key)[0]


def draw_recv_slots(key, part):
    return pair_tables(key)[1]


def touch_ends(result, key, smallest, top_value):
    longest = result.shape.index(max(result.shape))
    spots = []
    for shift in (0, 1):
        where = [jax.random.randint(jax.random.fold_in(key, axis), (), 0, length) for axis, length in enumerate(result.shape)]
        where[longest] = (where[longest] + shift) % result.shape[longest]
        spots.append(tuple(where))
    return result.at[spots[0]].set(smallest).at[spots[1]].set(top_value)


def strengthened(result, stream_key, source, target, blocks, factor):
    def block_of(axis_at):
        return (jnp.arange(result.shape[axis_at]) // (result.shape[axis_at] // blocks)).reshape((-1,) + (1,) * (result.ndim - 1 - axis_at))

    one_side = jax.random.permutation(stream_key, blocks)[block_of(target)]
    far = (block_of(target) + blocks // 2) % blocks
    return jnp.where((block_of(source) == one_side) | (block_of(source) == far), factor * result, result)


def block_scale(key, dims, shards, least, top_value):
    level = 1.0
    for axis_at, parts in shards:
        heights = jax.random.uniform(jax.random.fold_in(jax.random.fold_in(key, 6), axis_at), (parts,), jnp.float32, least / len(shards), top_value / len(shards))
        level = level * jnp.repeat(jnp.exp(heights), dims[axis_at] // parts).reshape((-1,) + (1,) * (len(dims) - 1 - axis_at))
    return level


def centred(stream_key, dims, deviation, bound, cuts=(), held_as=jnp.bfloat16):
    gain = block_scale(stream_key, dims, cuts, -0.22, 0.18) if cuts else 1.0
    result = jax.random.normal(stream_key, dims, jnp.float32) * deviation * gain
    return jnp.minimum(jnp.maximum(result, -bound), bound).astype(held_as)


def noise_with(own_key, extent, spread, reach, cuts, heavy, kind=jnp.bfloat16):
    array = spread * jax.random.normal(own_key, extent, jnp.float32)
    if cuts:
        array = array * block_scale(own_key, extent, cuts, -0.22, 0.18)
    return jnp.clip(strengthened(array, jax.random.fold_in(own_key, 3), *heavy), -reach, reach).astype(kind)


def setup_inputs(seed: int = 0, part: int = 0) -> dict:
    keys = jax.random.split(jax.random.key(seed), 9)
    own_keys = jax.random.split(jax.random.fold_in(keys[8], part), 9)
    base_heads = centred(own_keys[0], (TOKENS, HD), 1.0, 6.0, ((0, 4), (1, 4)))
    source_heads = centred(own_keys[1], (TOKENS, HD), 1.0, 6.0, ((0, 4), (1, 4)))
    residual = centred(own_keys[2], (TOKENS, D), 1.0, 6.0, ((0, 4), (1, 4)))
    weight = centred(keys[3], (HD, D), HD ** -0.5, 0.09375, ((0, 4), (1, 4)))
    cotangent = noise_with(own_keys[4], (TOKENS, D), 1.0, 6.0, ((0, 4),), (0, 1, 4, 2.0))
    send_slots = draw_send_slots(jax.random.fold_in(jax.random.fold_in(keys[8], part), 71), part)
    recv_slots = draw_recv_slots(jax.random.fold_in(jax.random.fold_in(keys[8], part), 71), part)
    head_mask = touch_ends((jax.random.randint(own_keys[7], (N_DP * PROMPTS_DEV, HEADS), 0, 2) < 1).astype(jnp.int32), jax.random.fold_in(own_keys[7], 1), 0, 1)
    return dict(base_heads=base_heads, source_heads=source_heads, residual=residual, weight=weight, cotangent=cotangent, send_slots=send_slots, recv_slots=recv_slots, head_mask=head_mask)


def reference(base_heads, source_heads, residual, weight, cotangent, send_slots, recv_slots, head_mask):
    live = send_slots >= 0
    sender = jnp.arange(N_DP, dtype=jnp.int32)[:, None, None]
    taker = jnp.arange(N_DP, dtype=jnp.int32)[None, :, None]
    src_glob = (sender * ROWS + jnp.maximum(send_slots, 0)).astype(jnp.int32)
    dst_glob = (taker * ROWS + jnp.transpose(recv_slots, (1, 0, 2))).astype(jnp.int32)
    target = jnp.where(live, dst_glob, TOKENS).reshape(-1).astype(jnp.int32)
    partner = jnp.zeros((TOKENS,), jnp.int32).at[target].set(src_glob.reshape(-1), mode="drop")
    paired = jnp.zeros((TOKENS,), jnp.int32).at[target].set(1, mode="drop")
    mask_rows = jnp.repeat(jnp.repeat(head_mask, PROMPT, axis=0), HDIM, axis=1)
    choose = (paired[:, None] == 1) & (mask_rows == 1)
    mixed = jnp.where(choose, source_heads[partner], base_heads)
    block = HD // N_TENSOR
    attn = jnp.zeros((TOKENS, D), jnp.float32)
    for q in range(N_TENSOR):
        part = jnp.dot(mixed[:, q * block:(q + 1) * block], weight[q * block:(q + 1) * block], preferred_element_type=jnp.float32)
        part = lax.optimization_barrier(part.astype(jnp.bfloat16))
        attn = attn + part.astype(jnp.float32)
    layer_out = (attn + residual.astype(jnp.float32)).astype(jnp.bfloat16)
    grad_mixed = lax.dot_general(cotangent, weight, (((1,), (1,)), ((), ())), preferred_element_type=jnp.float32).astype(jnp.bfloat16)
    zero = jnp.zeros_like(grad_mixed)
    grad_base = jnp.where(choose, zero, grad_mixed)
    back = jnp.where(paired == 1, partner, TOKENS).astype(jnp.int32)
    grad_source = jnp.zeros_like(grad_mixed).at[back].add(jnp.where(choose, grad_mixed, zero), mode="drop")
    mixed_blocks = mixed.reshape(N_DP, ROWS, HD)
    cot_blocks = cotangent.reshape(N_DP, ROWS, D)

    def add_term(total, pieces):
        term = lax.dot_general(pieces[0], pieces[1], (((0,), (0,)), ((), ())), preferred_element_type=jnp.float32)
        term = lax.optimization_barrier(term.astype(jnp.bfloat16))
        return total + term.astype(jnp.float32), None

    grad_weight, unused = lax.scan(add_term, jnp.zeros((HD, D), jnp.float32), (mixed_blocks, cot_blocks))
    return layer_out, grad_base, grad_source, grad_weight
```

```python
import functools

import jax
import jax.numpy as jnp
from jax import lax
from jax.experimental import pallas as pl
from jax.experimental.pallas import tpu as pltpu
from jax.sharding import PartitionSpec as P


def with_collectives(
    base_heads, source_heads, residual, weight, cotangent, send_slots, recv_slots, head_mask
):
    rows, width = base_heads.shape
    peers = send_slots.shape[1]
    slots = send_slots.shape[2]
    prompts, heads_here = head_mask.shape
    head_size = width // heads_here
    prompt_len = rows // prompts
    send_index = send_slots.reshape(-1)
    send_live = send_index >= 0
    outgoing = jnp.where(
        send_live[:, None], source_heads[jnp.maximum(send_index, 0)], jnp.zeros((), jnp.bfloat16)
    )
    arrived = lax.all_to_all(
        outgoing.reshape(peers, slots, width), "dp", split_axis=0, concat_axis=0, tiled=True
    ).reshape(peers * slots, width)
    recv_index = recv_slots.reshape(-1)
    recv_live = recv_index >= 0
    target = jnp.where(recv_live, recv_index, rows)
    incoming = jnp.zeros((rows, width), jnp.bfloat16).at[target].set(arrived, mode="drop")
    paired = jnp.zeros((rows,), jnp.int32).at[target].set(1, mode="drop")
    mask_rows = jnp.repeat(jnp.repeat(head_mask, prompt_len, axis=0), head_size, axis=1)
    choose = (paired[:, None] == 1) & (mask_rows == 1)
    mixed = jnp.where(choose, incoming, base_heads)
    partial_sum = jnp.dot(
        mixed, lax.all_gather(weight, "dp", axis=1, tiled=True), preferred_element_type=jnp.float32
    )
    attn = lax.psum_scatter(
        partial_sum.astype(jnp.bfloat16), "tensor", scatter_dimension=1, tiled=True
    ).astype(jnp.float32)
    layer_out = (attn + residual.astype(jnp.float32)).astype(jnp.bfloat16)
    grad_wide = lax.dot_general(
        cotangent,
        lax.all_gather(weight, "dp", axis=1, tiled=True),
        (((1,), (1,)), ((), ())),
        preferred_element_type=jnp.float32,
    )
    grad_mixed = grad_wide.astype(jnp.bfloat16)
    zero = jnp.zeros((), jnp.bfloat16)
    grad_base = jnp.where(choose, zero, grad_mixed)
    back_rows = jnp.where(recv_live, recv_index, 0)
    returned = jnp.where(recv_live[:, None] & choose[back_rows], grad_mixed[back_rows], zero)
    homeward = lax.all_to_all(
        returned.reshape(peers, slots, width), "dp", split_axis=0, concat_axis=0, tiled=True
    ).reshape(peers * slots, width)
    source_target = jnp.where(send_live, send_index, rows)
    grad_source = (
        jnp.zeros((rows, width), jnp.bfloat16).at[source_target].add(homeward, mode="drop")
    )
    grad_term = lax.dot_general(
        mixed, cotangent, (((0,), (0,)), ((), ())), preferred_element_type=jnp.float32
    )
    grad_weight = lax.psum_scatter(
        grad_term.astype(jnp.bfloat16), "dp", scatter_dimension=1, tiled=True
    ).astype(jnp.float32)
    return (layer_out, grad_base, grad_source, grad_weight)


MESH = pl.DeviceIdType.MESH
TILE = 256


def nn(a, b):
    return jnp.dot(a, b, preferred_element_type=jnp.float32)


def nt(a, b):
    return lax.dot_general(a, b, (((1,), (1,)), ((), ())), preferred_element_type=jnp.float32)


def tn(a, b):
    return lax.dot_general(a, b, (((0,), (0,)), ((), ())), preferred_element_type=jnp.float32)


def fused(
    n,
    weight_ref,
    cotangent_ref,
    residual_ref,
    base_ref,
    source_ref,
    choose_ref,
    pick_ref,
    place_ref,
    pick_back_ref,
    place_back_ref,
    layer_ref,
    grad_base_ref,
    grad_source_ref,
    grad_weight_ref,
    w_all,
    cot_own,
    cot_all,
    mixed_all,
    rows_out,
    rows_in,
    home_ref,
    part_out,
    part_in,
    grad_acc,
    res_v,
    local_sem,
    w_send,
    w_recv,
    y_send,
    y_recv,
    m_send,
    m_recv,
    s_send,
    s_recv,
    h_send,
    h_recv,
    c_send,
    c_recv,
    b_send,
    p_send,
    p_recv,
):
    g = lax.axis_index("group")
    i = lax.axis_index("dp")
    t = lax.axis_index("tensor")
    tokens, width = base_ref.shape
    half = w_all.shape[1] // 2
    block = w_all.shape[2]
    slots = rows_out.shape[0] // n
    quarter = tokens // n

    def remote(src, dst, send, recv, to):
        return pltpu.make_async_remote_copy(
            src_ref=src, dst_ref=dst, send_sem=send, recv_sem=recv, device_id=to, device_id_type=MESH
        )

    def columns(k):
        return pl.ds(pl.multiple_of(k * TILE, TILE), TILE)

    def mine():
        return pl.ds(pl.multiple_of(g * half, half), half)

    def theirs():
        return pl.ds(pl.multiple_of((1 - g) * half, half), half)

    def strip(k):
        return pl.ds(pl.multiple_of(k * quarter, quarter), quarter)

    def slot_rows(k):
        return pl.ds(pl.multiple_of(k * slots, slots), slots)

    def w_first(side):
        to = jnp.clip(i + 1 - 2 * side, 0, n - 1)
        return remote(
            weight_ref.at[mine(), :], w_all.at[i, mine(), :], w_send.at[side, i], w_recv.at[i], {"dp": to}
        )

    def w_pass(side, s):
        to = jnp.clip(i + 1 - 2 * side, 0, n - 1)
        return remote(
            w_all.at[s, mine(), :], w_all.at[s, mine(), :], w_send.at[side, s], w_recv.at[s], {"dp": to}
        )

    def w_across(s):
        return remote(
            w_all.at[s, mine(), :], w_all.at[s, mine(), :], y_send.at[s], y_recv.at[s], {"group": 1 - g}
        )

    def w_across_in(s):
        return remote(
            w_all.at[s, theirs(), :], w_all.at[s, theirs(), :], y_send.at[s], y_recv.at[s], {"group": 1 - g}
        )

    def m_pass(side, s):
        to = jnp.clip(i + 1 - 2 * side, 0, n - 1)
        return remote(mixed_all.at[s], mixed_all.at[s], m_send.at[side, s], m_recv.at[s], {"dp": to})

    def rows_to(j):
        return remote(rows_out.at[slot_rows(j), :], rows_in.at[slot_rows(i), :], s_send.at[j], s_recv.at[i], {"dp": j})

    def rows_from(j):
        return remote(rows_out.at[slot_rows(j), :], rows_in.at[slot_rows(j), :], s_send.at[j], s_recv.at[j], {"dp": j})

    def rows_home(j):
        return remote(rows_out.at[slot_rows(j), :], home_ref.at[slot_rows(i), :], h_send.at[j], h_recv.at[i], {"dp": j})

    def rows_home_in(j):
        return remote(rows_out.at[slot_rows(j), :], home_ref.at[slot_rows(j), :], h_send.at[j], h_recv.at[j], {"dp": j})

    def cot_to(j):
        where = pl.ds(pl.multiple_of(j * block, block), block)
        return remote(
            cotangent_ref.at[strip(t), where], cot_all.at[i, strip(t), :], c_send.at[j], c_recv.at[i, t], {"dp": j}
        )

    def cot_share(j, u):
        return remote(
            cot_all.at[j, strip(t), :], cot_all.at[j, strip(t), :], b_send.at[j, u], c_recv.at[j, t], {"tensor": u}
        )

    def cot_in(j, u):
        return remote(
            cot_all.at[j, strip(u), :], cot_all.at[j, strip(u), :], b_send.at[j, u], c_recv.at[j, u], {"tensor": u}
        )

    def part_to(u):
        return remote(part_out.at[u], part_in.at[t], p_send.at[u], p_recv.at[t], {"tensor": u})

    def part_from(u):
        return remote(part_out.at[u], part_in.at[u], p_send.at[u], p_recv.at[u], {"tensor": u})

    def others(me, body):
        def step(k, carry):
            body(lax.rem(me + k, n))
            return carry

        lax.fori_loop(1, n, step, 0)

    def at_distance(k, body):
        for side in range(2):
            s = i - k if side == 0 else i + k
            inside = (s >= 0) & (s < n)
            onward = inside & ((i + 1 < n) if side == 0 else (i >= 1))
            body(side, jnp.clip(s, 0, n - 1), inside, onward)

    loads = [pltpu.make_async_copy(weight_ref, w_all.at[i], local_sem.at[0])]
    for k in range(n):
        loads.append(
            pltpu.make_async_copy(
                cotangent_ref.at[:, k * block : (k + 1) * block], cot_own.at[k], local_sem.at[1 + k]
            )
        )
    loads.append(pltpu.make_async_copy(residual_ref, res_v, local_sem.at[1 + n]))
    for load in loads:
        load.start()

    barrier = pltpu.get_barrier_semaphore()
    others(i, lambda j: pl.semaphore_signal(barrier, inc=1, device_id={"dp": j}, device_id_type=MESH))
    others(t, lambda u: pl.semaphore_signal(barrier, inc=1, device_id={"tensor": u}, device_id_type=MESH))
    pl.semaphore_signal(barrier, inc=1, device_id={"group": 1 - g}, device_id_type=MESH)

    @pl.loop(0, width // TILE)
    def _(k):
        rows_out[:, columns(k)] = nn(pick_ref[...], source_ref[:, columns(k)]).astype(jnp.bfloat16)

    pl.semaphore_wait(barrier, 2 * (n - 1) + 1)

    others(i, lambda j: rows_to(j).start())

    def start_w(side, s, inside, onward):
        @pl.when(onward)
        def _():
            w_first(side).start()

    at_distance(0, start_w)
    others(i, lambda j: cot_to(j).start())
    rows_in[slot_rows(i), :] = rows_out[slot_rows(i), :]

    others(i, lambda j: rows_from(j).wait_recv())

    @pl.loop(0, width // TILE)
    def _(k):
        c = columns(k)
        incoming = nn(place_ref[...], rows_in[:, c])
        chosen = choose_ref[:, c].astype(jnp.float32) > 0.5
        mixed_all[i, :, c] = jnp.where(chosen, incoming, base_ref[:, c].astype(jnp.float32)).astype(jnp.bfloat16)
        grad_acc[:, c] = jnp.zeros((tokens, TILE), jnp.float32)

    def share_cot(j):
        cot_to(j).wait_send()
        cot_in(j, t).wait_recv()
        others(t, lambda u: cot_share(j, u).start())

    others(i, share_cot)
    for load in loads:
        load.wait()

    def use_weight(s):
        @pl.loop(0, width // TILE)
        def _(k):
            c = columns(k)
            part_out[s, :, c] = nn(mixed_all[i], w_all[s, :, c]).astype(jnp.bfloat16)
            grad_acc[:, c] += nt(cot_own[s], w_all[s, c, :])

        @pl.when(s != t)
        def _():
            part_to(s).start()

    def use_tokens(j):
        @pl.loop(0, width // TILE)
        def _(k):
            c = columns(k)
            grad_weight_ref[c, :] += tn(mixed_all[j, :, c], cot_all[j])

    def round_of(k, carry):
        def w_arrives(side, s, inside, onward):
            @pl.when(inside & (k < n))
            def _():
                w_pass(side, s).wait_recv()
                w_across(s).start()

                @pl.when(onward)
                def _():
                    w_pass(side, s).start()

        def m_arrives(side, s, inside, onward):
            @pl.when(inside & (k >= 2))
            def _():
                m_pass(side, s).wait_recv()

            @pl.when(onward)
            def _():
                m_pass(side, s).start()

        def w_used(side, s, inside, onward):
            first = inside if side == 0 else inside & (k >= 2)

            @pl.when(first)
            def _():
                @pl.when(k >= 2)
                def _():
                    w_across_in(s).wait_recv()

                use_weight(s)

        at_distance(k, w_arrives)

        @pl.when(k < n)
        def _():
            at_distance(k - 1, m_arrives)

        at_distance(k - 1, w_used)
        return carry

    lax.fori_loop(1, n + 1, round_of, 0)

    others(i, lambda j: rows_to(j).wait_send())

    @pl.loop(0, width // TILE)
    def _(k):
        c = columns(k)
        chosen = choose_ref[:, c].astype(jnp.float32) > 0.5
        grad = grad_acc[:, c]
        zero = jnp.zeros_like(grad)
        grad_base_ref[:, c] = jnp.where(chosen, zero, grad).astype(jnp.bfloat16)
        swapped = jnp.where(chosen, grad, zero).astype(jnp.bfloat16)
        rows_out[:, c] = nn(pick_back_ref[...], swapped).astype(jnp.bfloat16)

    others(i, lambda j: rows_home(j).start())
    home_ref[slot_rows(i), :] = rows_out[slot_rows(i), :]

    @pl.loop(0, width // TILE)
    def _(k):
        grad_weight_ref[columns(k), :] = tn(mixed_all[i, :, columns(k)], cot_own[i])

    def tokens_of(k, carry):
        def m_used(side, s, inside, onward):
            @pl.when(inside)
            def _():
                @pl.when(k == n - 1)
                def _():
                    m_pass(side, s).wait_recv()

                others(t, lambda u: cot_in(s, u).wait_recv())
                use_tokens(s)

        at_distance(k, m_used)
        return carry

    lax.fori_loop(1, n, tokens_of, 0)

    others(t, lambda u: part_from(u).wait_recv())
    part_in[t] = part_out[t]

    @pl.loop(0, width // TILE)
    def _(k):
        c = columns(k)
        total = res_v[:, c].astype(jnp.float32)
        summed = part_in[0, :, c].astype(jnp.float32)
        for u in range(1, n):
            summed += part_in[u, :, c].astype(jnp.float32)
        layer_ref[:, c] = (summed + total).astype(jnp.bfloat16)

    others(i, lambda j: rows_home_in(j).wait_recv())

    @pl.loop(0, width // TILE)
    def _(k):
        c = columns(k)
        grad_source_ref[:, c] = nn(place_back_ref[...], home_ref[:, c]).astype(jnp.bfloat16)

    others(i, lambda j: rows_home(j).wait_send())
    others(t, lambda u: part_to(u).wait_send())
    others(i, lambda j: others(t, lambda u: cot_share(j, u).wait_send()))

    def drain(k, carry):
        def sent(side, s, inside, onward):
            @pl.when(onward)
            def _():
                w_pass(side, s).wait_send()
                m_pass(side, s).wait_send()

            @pl.when(inside & (k >= 1))
            def _():
                w_across(s).wait_send()

        at_distance(k, sent)
        return carry

    lax.fori_loop(0, n, drain, 0)


def with_kernel(
    base_heads, source_heads, residual, weight, cotangent, send_slots, recv_slots, head_mask
):
    rows, width = base_heads.shape
    n = send_slots.shape[1]
    slots = n * send_slots.shape[2]
    depth, block = weight.shape
    prompts, heads_here = head_mask.shape
    send_index = send_slots.reshape(-1)
    recv_index = recv_slots.reshape(-1)
    row = jnp.arange(rows, dtype=jnp.int32)
    pick = (send_index[:, None] == row[None, :]).astype(jnp.bfloat16)
    place_back = (row[:, None] == send_index[None, :]).astype(jnp.bfloat16)
    place = (row[:, None] == recv_index[None, :]).astype(jnp.bfloat16)
    pick_back = (recv_index[:, None] == row[None, :]).astype(jnp.bfloat16)
    paired = jnp.any(row[:, None] == recv_index[None, :], axis=1)
    swap = (paired.reshape(prompts, rows // prompts)[:, :, None] & (head_mask == 1)[:, None, :]).reshape(
        rows, heads_here
    )
    choose = jnp.repeat(swap, width // heads_here, axis=1).astype(jnp.bfloat16)
    kept = pl.BlockSpec(memory_space=pl.ANY)
    near = pl.BlockSpec(memory_space=pltpu.VMEM)
    dma = pltpu.SemaphoreType.DMA
    bf16 = jnp.bfloat16
    return pl.pallas_call(
        functools.partial(fused, n),
        out_shape=(
            jax.ShapeDtypeStruct((rows, width), bf16),
            jax.ShapeDtypeStruct((rows, width), bf16),
            jax.ShapeDtypeStruct((rows, width), bf16),
            jax.ShapeDtypeStruct((depth, block), jnp.float32),
        ),
        in_specs=[kept] * 3 + [near] * 7,
        out_specs=(near,) * 4,
        scratch_shapes=[
            pltpu.VMEM((n, depth, block), bf16),
            pltpu.VMEM((n, rows, block), bf16),
            pltpu.VMEM((n, rows, block), bf16),
            pltpu.VMEM((n, rows, width), bf16),
            pltpu.VMEM((slots, width), bf16),
            pltpu.VMEM((slots, width), bf16),
            pltpu.VMEM((slots, width), bf16),
            pltpu.VMEM((n, rows, block), bf16),
            pltpu.VMEM((n, rows, block), bf16),
            pltpu.VMEM((rows, width), jnp.float32),
            pltpu.VMEM((rows, width), bf16),
            dma((n + 2,)),
            dma((2, n)),
            dma((n,)),
            dma((n,)),
            dma((n,)),
            dma((2, n)),
            dma((n,)),
            dma((n,)),
            dma((n,)),
            dma((n,)),
            dma((n,)),
            dma((n,)),
            dma((n, n)),
            dma((n, n)),
            dma((n,)),
            dma((n,)),
        ],
        compiler_params=pltpu.CompilerParams(
            collective_id=0, has_side_effects=True, vmem_limit_bytes=60 * 1024 * 1024
        ),
    )(
        weight, cotangent, residual, base_heads, source_heads, choose, pick, place, pick_back, place_back
    )


def solution(mesh):
    square = mesh.shape["dp"] == mesh.shape["tensor"] and mesh.shape["group"] == 2
    return jax.shard_map(
        with_kernel if square else with_collectives,
        mesh=mesh,
        in_specs=(
            P(("group", "dp"), "tensor"),
            P(("group", "dp"), "tensor"),
            P(("group", "dp"), "tensor"),
            P("tensor", "dp"),
            P(("group", "dp"), None),
            P(("group", "dp"), None, None),
            P(("group", "dp"), None, None),
            P(("group", "dp"), "tensor"),
        ),
        out_specs=(
            P(("group", "dp"), "tensor"),
            P(("group", "dp"), "tensor"),
            P(("group", "dp"), "tensor"),
            P(("group", "tensor"), "dp"),
        ),
        check_vma=False,
    )
```

```python
import functools

import jax
import jax.numpy as jnp
from jax import lax
from jax.experimental import pallas as pl
from jax.experimental.pallas import tpu as pltpu
from jax.sharding import PartitionSpec as P


def with_collectives(
    base_heads, source_heads, residual, weight, cotangent, send_slots, recv_slots, head_mask
):
    rows, width = base_heads.shape
    peers = send_slots.shape[1]
    slots = send_slots.shape[2]
    prompts, heads_here = head_mask.shape
    head_size = width // heads_here
    prompt_len = rows // prompts
    send_index = send_slots.reshape(-1)
    send_live = send_index >= 0
    outgoing = jnp.where(
        send_live[:, None], source_heads[jnp.maximum(send_index, 0)], jnp.zeros((), jnp.bfloat16)
    )
    arrived = lax.all_to_all(
        outgoing.reshape(peers, slots, width), "dp", split_axis=0, concat_axis=0, tiled=True
    ).reshape(peers * slots, width)
    recv_index = recv_slots.reshape(-1)
    recv_live = recv_index >= 0
    target = jnp.where(recv_live, recv_index, rows)
    incoming = jnp.zeros((rows, width), jnp.bfloat16).at[target].set(arrived, mode="drop")
    paired = jnp.zeros((rows,), jnp.int32).at[target].set(1, mode="drop")
    mask_rows = jnp.repeat(jnp.repeat(head_mask, prompt_len, axis=0), head_size, axis=1)
    choose = (paired[:, None] == 1) & (mask_rows == 1)
    mixed = jnp.where(choose, incoming, base_heads)
    partial_sum = jnp.dot(
        mixed, lax.all_gather(weight, "dp", axis=1, tiled=True), preferred_element_type=jnp.float32
    )
    attn = lax.psum_scatter(
        partial_sum.astype(jnp.bfloat16), "tensor", scatter_dimension=1, tiled=True
    ).astype(jnp.float32)
    layer_out = (attn + residual.astype(jnp.float32)).astype(jnp.bfloat16)
    grad_wide = lax.dot_general(
        cotangent,
        lax.all_gather(weight, "dp", axis=1, tiled=True),
        (((1,), (1,)), ((), ())),
        preferred_element_type=jnp.float32,
    )
    grad_mixed = grad_wide.astype(jnp.bfloat16)
    zero = jnp.zeros((), jnp.bfloat16)
    grad_base = jnp.where(choose, zero, grad_mixed)
    back_rows = jnp.where(recv_live, recv_index, 0)
    returned = jnp.where(recv_live[:, None] & choose[back_rows], grad_mixed[back_rows], zero)
    homeward = lax.all_to_all(
        returned.reshape(peers, slots, width), "dp", split_axis=0, concat_axis=0, tiled=True
    ).reshape(peers * slots, width)
    source_target = jnp.where(send_live, send_index, rows)
    grad_source = (
        jnp.zeros((rows, width), jnp.bfloat16).at[source_target].add(homeward, mode="drop")
    )
    grad_term = lax.dot_general(
        mixed, cotangent, (((0,), (0,)), ((), ())), preferred_element_type=jnp.float32
    )
    grad_weight = lax.psum_scatter(
        grad_term.astype(jnp.bfloat16), "dp", scatter_dimension=1, tiled=True
    ).astype(jnp.float32)
    return (layer_out, grad_base, grad_source, grad_weight)


MESH = pl.DeviceIdType.MESH
TILE = 256


def nn(a, b):
    return jnp.dot(a, b, preferred_element_type=jnp.float32)


def nt(a, b):
    return lax.dot_general(a, b, (((1,), (1,)), ((), ())), preferred_element_type=jnp.float32)


def tn(a, b):
    return lax.dot_general(a, b, (((0,), (0,)), ((), ())), preferred_element_type=jnp.float32)


def fused(
    n,
    weight_ref,
    cotangent_ref,
    residual_ref,
    base_ref,
    source_ref,
    send_ref,
    recv_ref,
    heads_ref,
    layer_ref,
    grad_base_ref,
    grad_source_ref,
    grad_weight_ref,
    w_all,
    cot_own,
    cot_all,
    mixed_all,
    rows_out,
    rows_in,
    home_ref,
    part_out,
    part_in,
    grad_acc,
    res_v,
    choose_v,
    place_v,
    back_v,
    swapped_v,
    end_out,
    end_in,
    local_sem,
    w_send,
    w_recv,
    y_send,
    y_recv,
    m_send,
    m_recv,
    s_send,
    s_recv,
    h_send,
    h_recv,
    c_send,
    c_recv,
    b_send,
    p_send,
    p_recv,
    e_send,
    e_recv,
):
    g = lax.axis_index("group")
    i = lax.axis_index("dp")
    t = lax.axis_index("tensor")
    tokens, width = base_ref.shape
    half = w_all.shape[1] // 2
    block = w_all.shape[2]
    slots = rows_out.shape[0] // n
    quarter = tokens // n
    middle = (i >= 1) & (i <= n - 2)
    beside_end = (i == 1) | (i == n - 2)
    end = jnp.where(i <= 1, 0, n - 1)

    def remote(src, dst, send, recv, to):
        return pltpu.make_async_remote_copy(
            src_ref=src, dst_ref=dst, send_sem=send, recv_sem=recv, device_id=to, device_id_type=MESH
        )

    def columns(k):
        return pl.ds(pl.multiple_of(k * TILE, TILE), TILE)

    def mine():
        return pl.ds(pl.multiple_of(g * half, half), half)

    def theirs():
        return pl.ds(pl.multiple_of((1 - g) * half, half), half)

    def strip(k):
        return pl.ds(pl.multiple_of(k * quarter, quarter), quarter)

    def slot_rows(k):
        return pl.ds(pl.multiple_of(k * slots, slots), slots)

    def w_first(side):
        to = jnp.clip(i + 1 - 2 * side, 0, n - 1)
        return remote(
            weight_ref.at[mine(), :], w_all.at[i, mine(), :], w_send.at[side, i], w_recv.at[i], {"dp": to}
        )

    def w_pass(side, s):
        to = jnp.clip(i + 1 - 2 * side, 0, n - 1)
        return remote(
            w_all.at[s, mine(), :], w_all.at[s, mine(), :], w_send.at[side, s], w_recv.at[s], {"dp": to}
        )

    def w_across(s):
        return remote(
            w_all.at[s, mine(), :], w_all.at[s, mine(), :], y_send.at[s], y_recv.at[s], {"group": 1 - g}
        )

    def w_across_in(s):
        return remote(
            w_all.at[s, theirs(), :], w_all.at[s, theirs(), :], y_send.at[s], y_recv.at[s], {"group": 1 - g}
        )

    def m_pass(side, s):
        to = jnp.clip(i + 1 - 2 * side, 0, n - 1)
        return remote(mixed_all.at[s], mixed_all.at[s], m_send.at[side, s], m_recv.at[s], {"dp": to})

    def rows_to(j):
        return remote(rows_out.at[slot_rows(j), :], rows_in.at[slot_rows(i), :], s_send.at[j], s_recv.at[i], {"dp": j})

    def rows_from(j):
        return remote(rows_out.at[slot_rows(j), :], rows_in.at[slot_rows(j), :], s_send.at[j], s_recv.at[j], {"dp": j})

    def rows_home(j):
        return remote(rows_out.at[slot_rows(j), :], home_ref.at[slot_rows(i), :], h_send.at[j], h_recv.at[i], {"dp": j})

    def rows_home_in(j):
        return remote(rows_out.at[slot_rows(j), :], home_ref.at[slot_rows(j), :], h_send.at[j], h_recv.at[j], {"dp": j})

    def cot_to(b):
        kind = 0 if 0 < b < n - 1 else 1
        taker = min(max(b, 1), n - 2)
        return remote(
            cotangent_ref.at[strip(t), b * block : (b + 1) * block],
            cot_all.at[kind, i, strip(t), :],
            c_send.at[b],
            c_recv.at[kind, i, t],
            {"dp": taker},
        )

    def cot_sent(body):
        for b in range(n):
            taker = min(max(b, 1), n - 2)

            @pl.when((i != b) & (i != taker))
            def _():
                body(cot_to(b))

    def cot_share(kind, j, u):
        piece = cot_all.at[kind, j, strip(t), :]
        return remote(piece, piece, b_send.at[kind, j, u], c_recv.at[kind, j, t], {"tensor": u})

    def cot_in(kind, j, u):
        piece = cot_all.at[kind, j, strip(u), :]
        return remote(piece, piece, b_send.at[kind, j, u], c_recv.at[kind, j, u], {"tensor": u})

    def end_pass():
        return remote(end_out, end_in, e_send.at[0], e_recv.at[0], {"dp": end})

    def part_to(u):
        return remote(part_out.at[u], part_in.at[t], p_send.at[u], p_recv.at[t], {"tensor": u})

    def part_from(u):
        return remote(part_out.at[u], part_in.at[u], p_send.at[u], p_recv.at[u], {"tensor": u})

    def others(me, body):
        def step(k, carry):
            body(lax.rem(me + k, n))
            return carry

        lax.fori_loop(1, n, step, 0)

    def at_distance(k, body):
        for side in range(2):
            s = i - k if side == 0 else i + k
            inside = (s >= 0) & (s < n)
            onward = inside & ((i + 1 < n) if side == 0 else (i >= 1))
            body(side, jnp.clip(s, 0, n - 1), inside, onward)

    loads = [pltpu.make_async_copy(weight_ref, w_all.at[i], local_sem.at[0])]
    for k in range(n):
        loads.append(
            pltpu.make_async_copy(
                cotangent_ref.at[:, k * block : (k + 1) * block], cot_own.at[k], local_sem.at[1 + k]
            )
        )
    loads.append(pltpu.make_async_copy(residual_ref, res_v, local_sem.at[1 + n]))
    for load in loads:
        load.start()

    barrier = pltpu.get_barrier_semaphore()
    others(i, lambda j: pl.semaphore_signal(barrier, inc=1, device_id={"dp": j}, device_id_type=MESH))
    others(t, lambda u: pl.semaphore_signal(barrier, inc=1, device_id={"tensor": u}, device_id_type=MESH))
    pl.semaphore_signal(barrier, inc=1, device_id={"group": 1 - g}, device_id_type=MESH)

    def hot(index):
        count = place_v.shape[1]
        equal = lax.broadcasted_iota(jnp.int32, (tokens, count), 0) == index
        return jnp.where(equal, 1.0, 0.0)

    back_v[...] = hot(send_ref[...]).astype(jnp.bfloat16)

    @pl.loop(0, rows_out.shape[0] // TILE)
    def _(k):
        rows_out[columns(k), :] = tn(back_v[:, columns(k)], source_ref[...]).astype(jnp.bfloat16)

    pl.semaphore_wait(barrier, 2 * (n - 1) + 1)

    others(i, lambda j: rows_to(j).start())

    def start_w(side, s, inside, onward):
        @pl.when(onward)
        def _():
            w_first(side).start()

    at_distance(0, start_w)
    cot_sent(lambda copy: copy.start())
    rows_in[slot_rows(i), :] = rows_out[slot_rows(i), :]
    place = hot(recv_ref[...])
    place_v[...] = place.astype(jnp.bfloat16)
    paired = jnp.max(place, axis=1, keepdims=True)
    prompts = heads_ref.shape[0]
    length = tokens // prompts
    for p in range(prompts):
        rows = slice(p * length, (p + 1) * length)
        choose_v[rows, :] = (paired[rows, :] * heads_ref[p : p + 1, :]).astype(jnp.bfloat16)

    others(i, lambda j: rows_from(j).wait_recv())

    @pl.loop(0, width // TILE)
    def _(k):
        c = columns(k)
        incoming = nn(place_v[...], rows_in[:, c])
        chosen = choose_v[:, c].astype(jnp.float32) > 0.5
        mixed_all[i, :, c] = jnp.where(chosen, incoming, base_ref[:, c].astype(jnp.float32)).astype(jnp.bfloat16)
        grad_acc[:, c] = jnp.zeros((tokens, TILE), jnp.float32)

    def m_onward(side, inside):
        return inside & ((i + 1 <= n - 2) if side == 0 else (i - 1 >= 1))

    def start_m(side, s, inside, onward):
        @pl.when(m_onward(side, inside))
        def _():
            m_pass(side, s).start()

    at_distance(0, start_m)
    for load in loads:
        load.wait()

    def blocks_taken(body):
        for kind in range(2):

            @pl.when(middle if kind == 0 else beside_end)
            def _():
                def one(j):
                    if kind == 0:
                        body(kind, j)
                    else:

                        @pl.when(j != end)
                        def _():
                            body(kind, j)

                others(i, one)

    def share_cot(kind, j):
        cot_in(kind, j, t).wait_recv()
        others(t, lambda u: cot_share(kind, j, u).start())

    def use_weight(s):
        @pl.loop(0, width // TILE)
        def _(k):
            c = columns(k)
            part_out[s, :, c] = nn(mixed_all[i], w_all[s, :, c]).astype(jnp.bfloat16)
            grad_acc[:, c] += nt(cot_own[s], w_all[s, c, :])

        @pl.when(s != t)
        def _():
            part_to(s).start()

    def use_tokens(j):
        @pl.loop(0, width // TILE)
        def _(k):
            c = columns(k)
            grad_weight_ref[c, :] += tn(mixed_all[j, :, c], cot_all[0, j])

    def end_terms():
        blocks_taken(lambda kind, j: others(t, lambda u: cot_in(kind, j, u).wait_recv()))
        first = lax.rem(end + 1, n)
        second = lax.rem(end + 2, n)
        third = lax.rem(end + 3, n)
        cot_all[1, i] = cot_own[end]

        @pl.loop(0, width // TILE)
        def _(k):
            c = columns(k)
            total = tn(mixed_all[first, :, c], cot_all[1, first])
            total += tn(mixed_all[second, :, c], cot_all[1, second])
            total += tn(mixed_all[third, :, c], cot_all[1, third])
            end_out[c, :] = total.astype(jnp.bfloat16)

        end_pass().start()

    def w_used(side, s, inside, onward):
        @pl.when(inside)
        def _():
            w_across_in(s).wait_recv()
            use_weight(s)

    use_weight(i)

    def round_of(k, carry):
        def w_arrives(side, s, inside, onward):
            @pl.when(inside)
            def _():
                w_pass(side, s).wait_recv()
                w_across(s).start()

                @pl.when(onward)
                def _():
                    w_pass(side, s).start()

        def m_arrives(side, s, inside, onward):
            @pl.when(inside & middle)
            def _():
                m_pass(side, s).wait_recv()

                @pl.when(m_onward(side, inside))
                def _():
                    m_pass(side, s).start()

        at_distance(k, w_arrives)
        at_distance(k, m_arrives)

        @pl.when(k == 1)
        def _():
            blocks_taken(share_cot)

        @pl.when((k == n - 2) & beside_end)
        def _():
            end_terms()

        at_distance(k, w_used)
        return carry

    lax.fori_loop(1, n, round_of, 0)

    others(i, lambda j: rows_to(j).wait_send())

    @pl.loop(0, width // TILE)
    def _(k):
        c = columns(k)
        chosen = choose_v[:, c].astype(jnp.float32) > 0.5
        grad = grad_acc[:, c]
        zero = jnp.zeros_like(grad)
        grad_base_ref[:, c] = jnp.where(chosen, zero, grad).astype(jnp.bfloat16)
        swapped_v[:, c] = jnp.where(chosen, grad, zero).astype(jnp.bfloat16)

    @pl.loop(0, rows_out.shape[0] // TILE)
    def _(k):
        rows_out[columns(k), :] = tn(place_v[:, columns(k)], swapped_v[...]).astype(jnp.bfloat16)

    others(i, lambda j: rows_home(j).start())
    home_ref[slot_rows(i), :] = rows_out[slot_rows(i), :]

    @pl.loop(0, width // TILE)
    def _(k):
        grad_weight_ref[columns(k), :] = tn(mixed_all[i, :, columns(k)], cot_own[i])

    @pl.when(middle)
    def _():
        others(i, use_tokens)

    others(t, lambda u: part_from(u).wait_recv())
    part_in[t] = part_out[t]

    @pl.loop(0, width // TILE)
    def _(k):
        c = columns(k)
        total = res_v[:, c].astype(jnp.float32)
        summed = part_in[0, :, c].astype(jnp.float32)
        for u in range(1, n):
            summed += part_in[u, :, c].astype(jnp.float32)
        layer_ref[:, c] = (summed + total).astype(jnp.bfloat16)

    others(i, lambda j: rows_home_in(j).wait_recv())

    @pl.loop(0, width // TILE)
    def _(k):
        c = columns(k)
        grad_source_ref[:, c] = nn(back_v[...], home_ref[:, c]).astype(jnp.bfloat16)

    @pl.when(jnp.logical_not(middle))
    def _():
        end_pass().wait_recv()

        @pl.loop(0, width // TILE)
        def _(k):
            grad_weight_ref[columns(k), :] += end_in[columns(k), :].astype(jnp.float32)

    @pl.when(beside_end)
    def _():
        end_pass().wait_send()

    cot_sent(lambda copy: copy.wait_send())
    others(i, lambda j: rows_home(j).wait_send())
    others(t, lambda u: part_to(u).wait_send())
    blocks_taken(lambda kind, j: others(t, lambda u: cot_share(kind, j, u).wait_send()))

    def drain(k, carry):
        def sent(side, s, inside, onward):
            @pl.when(onward)
            def _():
                w_pass(side, s).wait_send()

            @pl.when(m_onward(side, inside) & (middle | (k == 0)))
            def _():
                m_pass(side, s).wait_send()

            @pl.when(inside & (k >= 1))
            def _():
                w_across(s).wait_send()

        at_distance(k, sent)
        return carry

    lax.fori_loop(0, n, drain, 0)


def copy_out(*refs):
    sem = refs[8]
    copies = [pltpu.make_async_copy(refs[k], refs[4 + k], sem.at[k]) for k in range(4)]
    for copy in copies:
        copy.start()
    for copy in copies:
        copy.wait()


def with_kernel(
    base_heads, source_heads, residual, weight, cotangent, send_slots, recv_slots, head_mask
):
    rows, width = base_heads.shape
    n = send_slots.shape[1]
    slots = n * send_slots.shape[2]
    depth, block = weight.shape
    prompts, heads_here = head_mask.shape
    heads = jnp.repeat(head_mask, width // heads_here, axis=1).astype(jnp.float32)
    kept = pl.BlockSpec(memory_space=pl.ANY)
    near = pl.BlockSpec(memory_space=pltpu.VMEM)
    dma = pltpu.SemaphoreType.DMA
    bf16 = jnp.bfloat16
    results = pl.pallas_call(
        functools.partial(fused, n),
        out_shape=(
            jax.ShapeDtypeStruct((rows, width), bf16),
            jax.ShapeDtypeStruct((rows, width), bf16),
            jax.ShapeDtypeStruct((rows, width), bf16),
            jax.ShapeDtypeStruct((depth, block), jnp.float32),
        ),
        in_specs=[kept] * 3 + [near] * 5,
        out_specs=(near,) * 4,
        scratch_shapes=[
            pltpu.VMEM((n, depth, block), bf16),
            pltpu.VMEM((n, rows, block), bf16),
            pltpu.VMEM((2, n, rows, block), bf16),
            pltpu.VMEM((n, rows, width), bf16),
            pltpu.VMEM((slots, width), bf16),
            pltpu.VMEM((slots, width), bf16),
            pltpu.VMEM((slots, width), bf16),
            pltpu.VMEM((n, rows, block), bf16),
            pltpu.VMEM((n, rows, block), bf16),
            pltpu.VMEM((rows, width), jnp.float32),
            pltpu.VMEM((rows, width), bf16),
            pltpu.VMEM((rows, width), bf16),
            pltpu.VMEM((rows, slots), bf16),
            pltpu.VMEM((rows, slots), bf16),
            pltpu.VMEM((rows, width), bf16),
            pltpu.VMEM((depth, block), bf16),
            pltpu.VMEM((depth, block), bf16),
            dma((n + 2,)),
            dma((2, n)),
            dma((n,)),
            dma((n,)),
            dma((n,)),
            dma((2, n)),
            dma((n,)),
            dma((n,)),
            dma((n,)),
            dma((n,)),
            dma((n,)),
            dma((n,)),
            dma((2, n, n)),
            dma((2, n, n)),
            dma((n,)),
            dma((n,)),
            dma((1,)),
            dma((1,)),
        ],
        compiler_params=pltpu.CompilerParams(
            collective_id=0, has_side_effects=True, vmem_limit_bytes=60 * 1024 * 1024
        ),
    )(
        weight,
        cotangent,
        residual,
        base_heads,
        source_heads,
        send_slots.reshape(1, slots),
        recv_slots.reshape(1, slots),
        heads,
    )
    return pl.pallas_call(
        copy_out,
        out_shape=tuple(jax.ShapeDtypeStruct(x.shape, x.dtype) for x in results),
        in_specs=[kept] * 4,
        out_specs=(kept,) * 4,
        scratch_shapes=[dma((4,))],
        compiler_params=pltpu.CompilerParams(vmem_limit_bytes=60 * 1024 * 1024),
    )(*results)


def solution(mesh):
    square = mesh.shape["dp"] == mesh.shape["tensor"] == 4 and mesh.shape["group"] == 2
    return jax.shard_map(
        with_kernel if square else with_collectives,
        mesh=mesh,
        in_specs=(
            P(("group", "dp"), "tensor"),
            P(("group", "dp"), "tensor"),
            P(("group", "dp"), "tensor"),
            P("tensor", "dp"),
            P(("group", "dp"), None),
            P(("group", "dp"), None, None),
            P(("group", "dp"), None, None),
            P(("group", "dp"), "tensor"),
        ),
        out_specs=(
            P(("group", "dp"), "tensor"),
            P(("group", "dp"), "tensor"),
            P(("group", "dp"), "tensor"),
            P(("group", "tensor"), "dp"),
        ),
        check_vma=False,
    )
```

```python
import functools

import jax
import jax.numpy as jnp
from jax import lax
from jax.experimental import pallas as pl
from jax.experimental.pallas import tpu as pltpu
from jax.sharding import PartitionSpec as P


def with_collectives(
    base_heads, source_heads, residual, weight, cotangent, send_slots, recv_slots, head_mask
):
    rows, width = base_heads.shape
    peers = send_slots.shape[1]
    slots = send_slots.shape[2]
    prompts, heads_here = head_mask.shape
    head_size = width // heads_here
    prompt_len = rows // prompts
    send_index = send_slots.reshape(-1)
    send_live = send_index >= 0
    outgoing = jnp.where(
        send_live[:, None], source_heads[jnp.maximum(send_index, 0)], jnp.zeros((), jnp.bfloat16)
    )
    arrived = lax.all_to_all(
        outgoing.reshape(peers, slots, width), "dp", split_axis=0, concat_axis=0, tiled=True
    ).reshape(peers * slots, width)
    recv_index = recv_slots.reshape(-1)
    recv_live = recv_index >= 0
    target = jnp.where(recv_live, recv_index, rows)
    incoming = jnp.zeros((rows, width), jnp.bfloat16).at[target].set(arrived, mode="drop")
    paired = jnp.zeros((rows,), jnp.int32).at[target].set(1, mode="drop")
    mask_rows = jnp.repeat(jnp.repeat(head_mask, prompt_len, axis=0), head_size, axis=1)
    choose = (paired[:, None] == 1) & (mask_rows == 1)
    mixed = jnp.where(choose, incoming, base_heads)
    partial_sum = jnp.dot(
        mixed, lax.all_gather(weight, "dp", axis=1, tiled=True), preferred_element_type=jnp.float32
    )
    attn = lax.psum_scatter(
        partial_sum.astype(jnp.bfloat16), "tensor", scatter_dimension=1, tiled=True
    ).astype(jnp.float32)
    layer_out = (attn + residual.astype(jnp.float32)).astype(jnp.bfloat16)
    grad_wide = lax.dot_general(
        cotangent,
        lax.all_gather(weight, "dp", axis=1, tiled=True),
        (((1,), (1,)), ((), ())),
        preferred_element_type=jnp.float32,
    )
    grad_mixed = grad_wide.astype(jnp.bfloat16)
    zero = jnp.zeros((), jnp.bfloat16)
    grad_base = jnp.where(choose, zero, grad_mixed)
    back_rows = jnp.where(recv_live, recv_index, 0)
    returned = jnp.where(recv_live[:, None] & choose[back_rows], grad_mixed[back_rows], zero)
    homeward = lax.all_to_all(
        returned.reshape(peers, slots, width), "dp", split_axis=0, concat_axis=0, tiled=True
    ).reshape(peers * slots, width)
    source_target = jnp.where(send_live, send_index, rows)
    grad_source = (
        jnp.zeros((rows, width), jnp.bfloat16).at[source_target].add(homeward, mode="drop")
    )
    grad_term = lax.dot_general(
        mixed, cotangent, (((0,), (0,)), ((), ())), preferred_element_type=jnp.float32
    )
    grad_weight = lax.psum_scatter(
        grad_term.astype(jnp.bfloat16), "dp", scatter_dimension=1, tiled=True
    ).astype(jnp.float32)
    return (layer_out, grad_base, grad_source, grad_weight)


MESH = pl.DeviceIdType.MESH
TILE = 256


def nn(a, b):
    return jnp.dot(a, b, preferred_element_type=jnp.float32)


def nt(a, b):
    return lax.dot_general(a, b, (((1,), (1,)), ((), ())), preferred_element_type=jnp.float32)


def tn(a, b):
    return lax.dot_general(a, b, (((0,), (0,)), ((), ())), preferred_element_type=jnp.float32)


def fused(
    n,
    weight_ref,
    cotangent_ref,
    residual_ref,
    base_ref,
    source_ref,
    send_ref,
    recv_ref,
    heads_ref,
    layer_ref,
    grad_base_ref,
    grad_source_ref,
    grad_weight_ref,
    w_all,
    cot_own,
    cot_all,
    mixed_all,
    rows_out,
    rows_in,
    home_ref,
    part_out,
    part_in,
    grad_acc,
    res_v,
    choose_v,
    place_v,
    back_v,
    swapped_v,
    end_out,
    end_in,
    local_sem,
    w_send,
    w_recv,
    y_send,
    y_recv,
    m_send,
    m_recv,
    s_send,
    s_recv,
    h_send,
    h_recv,
    c_send,
    c_recv,
    b_send,
    p_send,
    p_recv,
    e_send,
    e_recv,
):
    g = lax.axis_index("group")
    i = lax.axis_index("dp")
    t = lax.axis_index("tensor")
    tokens, width = base_ref.shape
    half = w_all.shape[1] // 2
    block = w_all.shape[2]
    slots = rows_out.shape[0] // n
    quarter = tokens // n
    middle = (i >= 1) & (i <= n - 2)
    beside_end = (i == 1) | (i == n - 2)
    end = jnp.where(i <= 1, 0, n - 1)

    def remote(src, dst, send, recv, to):
        return pltpu.make_async_remote_copy(
            src_ref=src, dst_ref=dst, send_sem=send, recv_sem=recv, device_id=to, device_id_type=MESH
        )

    def columns(k):
        return pl.ds(pl.multiple_of(k * TILE, TILE), TILE)

    def mine():
        return pl.ds(pl.multiple_of(g * half, half), half)

    def theirs():
        return pl.ds(pl.multiple_of((1 - g) * half, half), half)

    def strip(k):
        return pl.ds(pl.multiple_of(k * quarter, quarter), quarter)

    def slot_rows(k):
        return pl.ds(pl.multiple_of(k * slots, slots), slots)

    def w_first(side):
        to = jnp.clip(i + 1 - 2 * side, 0, n - 1)
        return remote(
            weight_ref.at[mine(), :], w_all.at[i, mine(), :], w_send.at[side, i], w_recv.at[i], {"dp": to}
        )

    def w_pass(side, s):
        to = jnp.clip(i + 1 - 2 * side, 0, n - 1)
        return remote(
            w_all.at[s, mine(), :], w_all.at[s, mine(), :], w_send.at[side, s], w_recv.at[s], {"dp": to}
        )

    def w_across(s):
        return remote(
            w_all.at[s, mine(), :], w_all.at[s, mine(), :], y_send.at[s], y_recv.at[s], {"group": 1 - g}
        )

    def w_across_in(s):
        return remote(
            w_all.at[s, theirs(), :], w_all.at[s, theirs(), :], y_send.at[s], y_recv.at[s], {"group": 1 - g}
        )

    def m_pass(side, s):
        to = jnp.clip(i + 1 - 2 * side, 0, n - 1)
        return remote(mixed_all.at[s], mixed_all.at[s], m_send.at[side, s], m_recv.at[s], {"dp": to})

    def rows_to(j):
        return remote(rows_out.at[slot_rows(j), :], rows_in.at[slot_rows(i), :], s_send.at[j], s_recv.at[i], {"dp": j})

    def rows_from(j):
        return remote(rows_out.at[slot_rows(j), :], rows_in.at[slot_rows(j), :], s_send.at[j], s_recv.at[j], {"dp": j})

    def rows_home(j):
        return remote(rows_out.at[slot_rows(j), :], home_ref.at[slot_rows(i), :], h_send.at[j], h_recv.at[i], {"dp": j})

    def rows_home_in(j):
        return remote(rows_out.at[slot_rows(j), :], home_ref.at[slot_rows(j), :], h_send.at[j], h_recv.at[j], {"dp": j})

    def cot_to(b):
        kind = 0 if 0 < b < n - 1 else 1
        taker = min(max(b, 1), n - 2)
        return remote(
            cotangent_ref.at[strip(t), b * block : (b + 1) * block],
            cot_all.at[kind, i, strip(t), :],
            c_send.at[b],
            c_recv.at[kind, i, t],
            {"dp": taker},
        )

    def cot_sent(body, blocks):
        for b in blocks:
            taker = min(max(b, 1), n - 2)

            @pl.when((i != b) & (i != taker))
            def _():
                body(cot_to(b))

    def cot_share(kind, j, u):
        piece = cot_all.at[kind, j, strip(t), :]
        return remote(piece, piece, b_send.at[kind, j, u], c_recv.at[kind, j, t], {"tensor": u})

    def cot_in(kind, j, u):
        piece = cot_all.at[kind, j, strip(u), :]
        return remote(piece, piece, b_send.at[kind, j, u], c_recv.at[kind, j, u], {"tensor": u})

    def end_pass():
        return remote(end_out, end_in, e_send.at[0], e_recv.at[0], {"dp": end})

    def part_to(u):
        return remote(part_out.at[u], part_in.at[t], p_send.at[u], p_recv.at[t], {"tensor": u})

    def part_from(u):
        return remote(part_out.at[u], part_in.at[u], p_send.at[u], p_recv.at[u], {"tensor": u})

    def others(me, body):
        def step(k, carry):
            body(lax.rem(me + k, n))
            return carry

        lax.fori_loop(1, n, step, 0)

    def at_distance(k, body):
        for side in range(2):
            s = i - k if side == 0 else i + k
            inside = (s >= 0) & (s < n)
            onward = inside & ((i + 1 < n) if side == 0 else (i >= 1))
            body(side, jnp.clip(s, 0, n - 1), inside, onward)

    loads = [pltpu.make_async_copy(weight_ref, w_all.at[i], local_sem.at[0])]
    for k in range(n):
        loads.append(
            pltpu.make_async_copy(
                cotangent_ref.at[:, k * block : (k + 1) * block], cot_own.at[k], local_sem.at[1 + k]
            )
        )
    loads.append(pltpu.make_async_copy(residual_ref, res_v, local_sem.at[1 + n]))
    for load in loads:
        load.start()

    barrier = pltpu.get_barrier_semaphore()
    others(i, lambda j: pl.semaphore_signal(barrier, inc=1, device_id={"dp": j}, device_id_type=MESH))
    others(t, lambda u: pl.semaphore_signal(barrier, inc=1, device_id={"tensor": u}, device_id_type=MESH))
    pl.semaphore_signal(barrier, inc=1, device_id={"group": 1 - g}, device_id_type=MESH)

    def hot(index):
        count = place_v.shape[1]
        equal = lax.broadcasted_iota(jnp.int32, (tokens, count), 0) == index
        return jnp.where(equal, 1.0, 0.0)

    back_v[...] = hot(send_ref[...]).astype(jnp.bfloat16)

    @pl.loop(0, rows_out.shape[0] // TILE)
    def _(k):
        rows_out[columns(k), :] = tn(back_v[:, columns(k)], source_ref[...]).astype(jnp.bfloat16)

    pl.semaphore_wait(barrier, 2 * (n - 1) + 1)

    others(i, lambda j: rows_to(j).start())

    def start_w(side, s, inside, onward):
        @pl.when(onward)
        def _():
            w_first(side).start()

    at_distance(0, start_w)
    rows_in[slot_rows(i), :] = rows_out[slot_rows(i), :]
    place = hot(recv_ref[...])
    place_v[...] = place.astype(jnp.bfloat16)
    paired = jnp.max(place, axis=1, keepdims=True)
    prompts = heads_ref.shape[0]
    length = tokens // prompts
    for p in range(prompts):
        rows = slice(p * length, (p + 1) * length)
        choose_v[rows, :] = (paired[rows, :] * heads_ref[p : p + 1, :]).astype(jnp.bfloat16)

    others(i, lambda j: rows_from(j).wait_recv())

    @pl.loop(0, width // TILE)
    def _(k):
        c = columns(k)
        incoming = nn(place_v[...], rows_in[:, c])
        chosen = choose_v[:, c].astype(jnp.float32) > 0.5
        mixed_all[i, :, c] = jnp.where(chosen, incoming, base_ref[:, c].astype(jnp.float32)).astype(jnp.bfloat16)
        grad_acc[:, c] = jnp.zeros((tokens, TILE), jnp.float32)

    def m_onward(side, inside):
        return inside & ((i + 1 <= n - 2) if side == 0 else (i - 1 >= 1))

    def start_m(side, s, inside, onward):
        @pl.when(m_onward(side, inside))
        def _():
            m_pass(side, s).start()

    for load in loads:
        load.wait()

    def blocks_taken(kind, body):
        @pl.when(middle if kind == 0 else beside_end)
        def _():
            def one(j):
                if kind == 0:
                    body(kind, j)
                else:

                    @pl.when(j != end)
                    def _():
                        body(kind, j)

            others(i, one)

    def share_cot(kind, j):
        cot_in(kind, j, t).wait_recv()
        others(t, lambda u: cot_share(kind, j, u).start())

    def use_weight(s):
        @pl.loop(0, width // TILE)
        def _(k):
            c = columns(k)
            part_out[s, :, c] = nn(mixed_all[i], w_all[s, :, c]).astype(jnp.bfloat16)
            grad_acc[:, c] += nt(cot_own[s], w_all[s, c, :])

        @pl.when(s != t)
        def _():
            part_to(s).start()

    def use_tokens(j):
        others(t, lambda u: cot_in(0, j, u).wait_recv())

        @pl.loop(0, width // TILE)
        def _(k):
            c = columns(k)
            grad_weight_ref[c, :] += tn(mixed_all[j, :, c], cot_all[0, j])

    def end_terms():
        blocks_taken(1, lambda kind, j: others(t, lambda u: cot_in(kind, j, u).wait_recv()))
        first = lax.rem(end + 1, n)
        second = lax.rem(end + 2, n)
        third = lax.rem(end + 3, n)
        cot_all[1, i] = cot_own[end]

        @pl.loop(0, width // TILE)
        def _(k):
            c = columns(k)
            total = tn(mixed_all[first, :, c], cot_all[1, first])
            total += tn(mixed_all[second, :, c], cot_all[1, second])
            total += tn(mixed_all[third, :, c], cot_all[1, third])
            end_out[c, :] = total.astype(jnp.bfloat16)

        end_pass().start()

    def w_used(side, s, inside, onward):
        @pl.when(inside)
        def _():
            w_across_in(s).wait_recv()
            use_weight(s)

    def w_arrives(side, s, inside, onward):
        @pl.when(inside)
        def _():
            w_pass(side, s).wait_recv()

            @pl.when(onward)
            def _():
                w_pass(side, s).start()

            w_across(s).start()

    def m_arrives(side, s, inside, onward):
        @pl.when(inside & middle)
        def _():
            m_pass(side, s).wait_recv()

            @pl.when(m_onward(side, inside))
            def _():
                m_pass(side, s).start()

    at_distance(1, w_arrives)
    at_distance(0, start_m)
    cot_sent(lambda copy: copy.start(), (0, n - 1))
    use_weight(i)
    at_distance(2, w_arrives)
    at_distance(1, m_arrives)
    cot_sent(lambda copy: copy.start(), range(1, n - 1))
    at_distance(1, w_used)
    blocks_taken(1, share_cot)
    at_distance(3, w_arrives)
    at_distance(2, w_used)
    at_distance(2, m_arrives)

    @pl.when(beside_end)
    def _():
        end_terms()

    blocks_taken(0, share_cot)
    at_distance(3, w_used)

    others(i, lambda j: rows_to(j).wait_send())

    @pl.loop(0, width // TILE)
    def _(k):
        c = columns(k)
        chosen = choose_v[:, c].astype(jnp.float32) > 0.5
        grad = grad_acc[:, c]
        zero = jnp.zeros_like(grad)
        grad_base_ref[:, c] = jnp.where(chosen, zero, grad).astype(jnp.bfloat16)
        swapped_v[:, c] = jnp.where(chosen, grad, zero).astype(jnp.bfloat16)

    @pl.loop(0, rows_out.shape[0] // TILE)
    def _(k):
        rows_out[columns(k), :] = tn(place_v[:, columns(k)], swapped_v[...]).astype(jnp.bfloat16)

    others(i, lambda j: rows_home(j).start())
    home_ref[slot_rows(i), :] = rows_out[slot_rows(i), :]

    @pl.loop(0, width // TILE)
    def _(k):
        grad_weight_ref[columns(k), :] = tn(mixed_all[i, :, columns(k)], cot_own[i])

    @pl.when(middle)
    def _():
        others(i, use_tokens)

    others(t, lambda u: part_from(u).wait_recv())
    part_in[t] = part_out[t]

    @pl.loop(0, width // TILE)
    def _(k):
        c = columns(k)
        total = res_v[:, c].astype(jnp.float32)
        summed = part_in[0, :, c].astype(jnp.float32)
        for u in range(1, n):
            summed += part_in[u, :, c].astype(jnp.float32)
        layer_ref[:, c] = (summed + total).astype(jnp.bfloat16)

    others(i, lambda j: rows_home_in(j).wait_recv())

    @pl.loop(0, width // TILE)
    def _(k):
        c = columns(k)
        grad_source_ref[:, c] = nn(back_v[...], home_ref[:, c]).astype(jnp.bfloat16)

    @pl.when(jnp.logical_not(middle))
    def _():
        end_pass().wait_recv()

        @pl.loop(0, width // TILE)
        def _(k):
            grad_weight_ref[columns(k), :] += end_in[columns(k), :].astype(jnp.float32)

    @pl.when(beside_end)
    def _():
        end_pass().wait_send()

    cot_sent(lambda copy: copy.wait_send(), range(n))
    others(i, lambda j: rows_home(j).wait_send())
    others(t, lambda u: part_to(u).wait_send())
    for kind in range(2):
        blocks_taken(kind, lambda kind, j: others(t, lambda u: cot_share(kind, j, u).wait_send()))

    def drain(k, carry):
        def sent(side, s, inside, onward):
            @pl.when(onward)
            def _():
                w_pass(side, s).wait_send()

            @pl.when(m_onward(side, inside) & (middle | (k == 0)))
            def _():
                m_pass(side, s).wait_send()

            @pl.when(inside & (k >= 1))
            def _():
                w_across(s).wait_send()

        at_distance(k, sent)
        return carry

    lax.fori_loop(0, n, drain, 0)


def copy_out(*refs):
    for k in range(4):
        refs[4 + k][...] = refs[k][...]


def with_kernel(
    base_heads, source_heads, residual, weight, cotangent, send_slots, recv_slots, head_mask
):
    rows, width = base_heads.shape
    n = send_slots.shape[1]
    slots = n * send_slots.shape[2]
    depth, block = weight.shape
    prompts, heads_here = head_mask.shape
    heads = jnp.repeat(head_mask, width // heads_here, axis=1).astype(jnp.float32)
    kept = pl.BlockSpec(memory_space=pl.ANY)
    near = pl.BlockSpec(memory_space=pltpu.VMEM)
    dma = pltpu.SemaphoreType.DMA
    bf16 = jnp.bfloat16
    results = pl.pallas_call(
        functools.partial(fused, n),
        out_shape=(
            jax.ShapeDtypeStruct((rows, width), bf16),
            jax.ShapeDtypeStruct((rows, width), bf16),
            jax.ShapeDtypeStruct((rows, width), bf16),
            jax.ShapeDtypeStruct((depth, block), jnp.float32),
        ),
        in_specs=[kept] * 3 + [near] * 5,
        out_specs=(near,) * 4,
        scratch_shapes=[
            pltpu.VMEM((n, depth, block), bf16),
            pltpu.VMEM((n, rows, block), bf16),
            pltpu.VMEM((2, n, rows, block), bf16),
            pltpu.VMEM((n, rows, width), bf16),
            pltpu.VMEM((slots, width), bf16),
            pltpu.VMEM((slots, width), bf16),
            pltpu.VMEM((slots, width), bf16),
            pltpu.VMEM((n, rows, block), bf16),
            pltpu.VMEM((n, rows, block), bf16),
            pltpu.VMEM((rows, width), jnp.float32),
            pltpu.VMEM((rows, width), bf16),
            pltpu.VMEM((rows, width), bf16),
            pltpu.VMEM((rows, slots), bf16),
            pltpu.VMEM((rows, slots), bf16),
            pltpu.VMEM((rows, width), bf16),
            pltpu.VMEM((depth, block), bf16),
            pltpu.VMEM((depth, block), bf16),
            dma((n + 2,)),
            dma((2, n)),
            dma((n,)),
            dma((n,)),
            dma((n,)),
            dma((2, n)),
            dma((n,)),
            dma((n,)),
            dma((n,)),
            dma((n,)),
            dma((n,)),
            dma((n,)),
            dma((2, n, n)),
            dma((2, n, n)),
            dma((n,)),
            dma((n,)),
            dma((1,)),
            dma((1,)),
        ],
        compiler_params=pltpu.CompilerParams(
            collective_id=0, has_side_effects=True, vmem_limit_bytes=60 * 1024 * 1024
        ),
    )(
        weight,
        cotangent,
        residual,
        base_heads,
        source_heads,
        send_slots.reshape(1, slots),
        recv_slots.reshape(1, slots),
        heads,
    )
    steps = 4
    blocks = [pl.BlockSpec((x.shape[0] // steps, x.shape[1]), lambda k: (k, 0)) for x in results]
    return pl.pallas_call(
        copy_out,
        grid=(steps,),
        out_shape=tuple(jax.ShapeDtypeStruct(x.shape, x.dtype) for x in results),
        in_specs=blocks,
        out_specs=tuple(blocks),
        compiler_params=pltpu.CompilerParams(vmem_limit_bytes=60 * 1024 * 1024),
    )(*results)


def solution(mesh):
    square = mesh.shape["dp"] == mesh.shape["tensor"] == 4 and mesh.shape["group"] == 2
    return jax.shard_map(
        with_kernel if square else with_collectives,
        mesh=mesh,
        in_specs=(
            P(("group", "dp"), "tensor"),
            P(("group", "dp"), "tensor"),
            P(("group", "dp"), "tensor"),
            P("tensor", "dp"),
            P(("group", "dp"), None),
            P(("group", "dp"), None, None),
            P(("group", "dp"), None, None),
            P(("group", "dp"), "tensor"),
        ),
        out_specs=(
            P(("group", "dp"), "tensor"),
            P(("group", "dp"), "tensor"),
            P(("group", "dp"), "tensor"),
            P(("group", "tensor"), "dp"),
        ),
        check_vma=False,
    )
```

```python
import functools

import jax
import jax.numpy as jnp
from jax import lax
from jax.experimental import pallas as pl
from jax.experimental.pallas import tpu as pltpu
from jax.sharding import PartitionSpec as P


def with_collectives(
    base_heads, source_heads, residual, weight, cotangent, send_slots, recv_slots, head_mask
):
    rows, width = base_heads.shape
    peers = send_slots.shape[1]
    slots = send_slots.shape[2]
    prompts, heads_here = head_mask.shape
    head_size = width // heads_here
    prompt_len = rows // prompts
    send_index = send_slots.reshape(-1)
    send_live = send_index >= 0
    outgoing = jnp.where(
        send_live[:, None], source_heads[jnp.maximum(send_index, 0)], jnp.zeros((), jnp.bfloat16)
    )
    arrived = lax.all_to_all(
        outgoing.reshape(peers, slots, width), "dp", split_axis=0, concat_axis=0, tiled=True
    ).reshape(peers * slots, width)
    recv_index = recv_slots.reshape(-1)
    recv_live = recv_index >= 0
    target = jnp.where(recv_live, recv_index, rows)
    incoming = jnp.zeros((rows, width), jnp.bfloat16).at[target].set(arrived, mode="drop")
    paired = jnp.zeros((rows,), jnp.int32).at[target].set(1, mode="drop")
    mask_rows = jnp.repeat(jnp.repeat(head_mask, prompt_len, axis=0), head_size, axis=1)
    choose = (paired[:, None] == 1) & (mask_rows == 1)
    mixed = jnp.where(choose, incoming, base_heads)
    partial_sum = jnp.dot(
        mixed, lax.all_gather(weight, "dp", axis=1, tiled=True), preferred_element_type=jnp.float32
    )
    attn = lax.psum_scatter(
        partial_sum.astype(jnp.bfloat16), "tensor", scatter_dimension=1, tiled=True
    ).astype(jnp.float32)
    layer_out = (attn + residual.astype(jnp.float32)).astype(jnp.bfloat16)
    grad_wide = lax.dot_general(
        cotangent,
        lax.all_gather(weight, "dp", axis=1, tiled=True),
        (((1,), (1,)), ((), ())),
        preferred_element_type=jnp.float32,
    )
    grad_mixed = grad_wide.astype(jnp.bfloat16)
    zero = jnp.zeros((), jnp.bfloat16)
    grad_base = jnp.where(choose, zero, grad_mixed)
    back_rows = jnp.where(recv_live, recv_index, 0)
    returned = jnp.where(recv_live[:, None] & choose[back_rows], grad_mixed[back_rows], zero)
    homeward = lax.all_to_all(
        returned.reshape(peers, slots, width), "dp", split_axis=0, concat_axis=0, tiled=True
    ).reshape(peers * slots, width)
    source_target = jnp.where(send_live, send_index, rows)
    grad_source = (
        jnp.zeros((rows, width), jnp.bfloat16).at[source_target].add(homeward, mode="drop")
    )
    grad_term = lax.dot_general(
        mixed, cotangent, (((0,), (0,)), ((), ())), preferred_element_type=jnp.float32
    )
    grad_weight = lax.psum_scatter(
        grad_term.astype(jnp.bfloat16), "dp", scatter_dimension=1, tiled=True
    ).astype(jnp.float32)
    return (layer_out, grad_base, grad_source, grad_weight)


MESH = pl.DeviceIdType.MESH
TILE = 256


def nn(a, b):
    return jnp.dot(a, b, preferred_element_type=jnp.float32)


def nt(a, b):
    return lax.dot_general(a, b, (((1,), (1,)), ((), ())), preferred_element_type=jnp.float32)


def tn(a, b):
    return lax.dot_general(a, b, (((0,), (0,)), ((), ())), preferred_element_type=jnp.float32)


def fused(
    n,
    weight_ref,
    cotangent_ref,
    residual_ref,
    base_ref,
    source_ref,
    send_ref,
    recv_ref,
    heads_ref,
    layer_ref,
    grad_base_ref,
    grad_source_ref,
    grad_weight_ref,
    w_all,
    cot_own,
    cot_all,
    mixed_all,
    rows_out,
    rows_in,
    home_ref,
    part_out,
    part_in,
    grad_acc,
    res_v,
    choose_v,
    place_v,
    back_v,
    swapped_v,
    local_sem,
    w_send,
    w_recv,
    y_send,
    y_recv,
    m_send,
    m_recv,
    s_send,
    s_recv,
    h_send,
    h_recv,
    c_send,
    c_recv,
    b_send,
    p_send,
    p_recv,
):
    g = lax.axis_index("group")
    i = lax.axis_index("dp")
    t = lax.axis_index("tensor")
    tokens, width = base_ref.shape
    half = w_all.shape[1] // 2
    block = w_all.shape[2]
    slots = rows_out.shape[0] // n
    quarter = tokens // n

    def remote(src, dst, send, recv, to):
        return pltpu.make_async_remote_copy(
            src_ref=src, dst_ref=dst, send_sem=send, recv_sem=recv, device_id=to, device_id_type=MESH
        )

    def columns(k):
        return pl.ds(pl.multiple_of(k * TILE, TILE), TILE)

    def mine():
        return pl.ds(pl.multiple_of(g * half, half), half)

    def theirs():
        return pl.ds(pl.multiple_of((1 - g) * half, half), half)

    def strip(k):
        return pl.ds(pl.multiple_of(k * quarter, quarter), quarter)

    def slot_rows(k):
        return pl.ds(pl.multiple_of(k * slots, slots), slots)

    def w_first(side):
        to = jnp.clip(i + 1 - 2 * side, 0, n - 1)
        return remote(
            weight_ref.at[mine(), :], w_all.at[i, mine(), :], w_send.at[side, i], w_recv.at[i], {"dp": to}
        )

    def w_pass(side, s):
        to = jnp.clip(i + 1 - 2 * side, 0, n - 1)
        return remote(
            w_all.at[s, mine(), :], w_all.at[s, mine(), :], w_send.at[side, s], w_recv.at[s], {"dp": to}
        )

    def w_across(s):
        return remote(
            w_all.at[s, mine(), :], w_all.at[s, mine(), :], y_send.at[s], y_recv.at[s], {"group": 1 - g}
        )

    def w_across_in(s):
        return remote(
            w_all.at[s, theirs(), :], w_all.at[s, theirs(), :], y_send.at[s], y_recv.at[s], {"group": 1 - g}
        )

    def m_pass(side, s):
        to = jnp.clip(i + 1 - 2 * side, 0, n - 1)
        return remote(mixed_all.at[s], mixed_all.at[s], m_send.at[side, s], m_recv.at[s], {"dp": to})

    def rows_to(j):
        return remote(rows_out.at[slot_rows(j), :], rows_in.at[slot_rows(i), :], s_send.at[j], s_recv.at[i], {"dp": j})

    def rows_from(j):
        return remote(rows_out.at[slot_rows(j), :], rows_in.at[slot_rows(j), :], s_send.at[j], s_recv.at[j], {"dp": j})

    def rows_home(j):
        return remote(rows_out.at[slot_rows(j), :], home_ref.at[slot_rows(i), :], h_send.at[j], h_recv.at[i], {"dp": j})

    def rows_home_in(j):
        return remote(rows_out.at[slot_rows(j), :], home_ref.at[slot_rows(j), :], h_send.at[j], h_recv.at[j], {"dp": j})

    def cot_to(b):
        kind = 0
        taker = b
        return remote(
            cotangent_ref.at[strip(t), b * block : (b + 1) * block],
            cot_all.at[kind, i, strip(t), :],
            c_send.at[b],
            c_recv.at[kind, i, t],
            {"dp": taker},
        )

    def cot_sent(body, blocks):
        for b in blocks:

            @pl.when(i != b)
            def _():
                body(cot_to(b))

    def cot_share(kind, j, u):
        piece = cot_all.at[kind, j, strip(t), :]
        return remote(piece, piece, b_send.at[kind, j, u], c_recv.at[kind, j, t], {"tensor": u})

    def cot_in(kind, j, u):
        piece = cot_all.at[kind, j, strip(u), :]
        return remote(piece, piece, b_send.at[kind, j, u], c_recv.at[kind, j, u], {"tensor": u})

    def part_to(u):
        return remote(part_out.at[u], part_in.at[t], p_send.at[u], p_recv.at[t], {"tensor": u})

    def part_from(u):
        return remote(part_out.at[u], part_in.at[u], p_send.at[u], p_recv.at[u], {"tensor": u})

    def others(me, body):
        def step(k, carry):
            body(lax.rem(me + k, n))
            return carry

        lax.fori_loop(1, n, step, 0)

    def at_distance(k, body):
        for side in range(2):
            s = i - k if side == 0 else i + k
            inside = (s >= 0) & (s < n)
            onward = inside & ((i + 1 < n) if side == 0 else (i >= 1))
            body(side, jnp.clip(s, 0, n - 1), inside, onward)

    loads = [pltpu.make_async_copy(weight_ref, w_all.at[i], local_sem.at[0])]
    for k in range(n):
        loads.append(
            pltpu.make_async_copy(
                cotangent_ref.at[:, k * block : (k + 1) * block], cot_own.at[k], local_sem.at[1 + k]
            )
        )
    loads.append(pltpu.make_async_copy(residual_ref, res_v, local_sem.at[1 + n]))
    for load in loads:
        load.start()

    barrier = pltpu.get_barrier_semaphore()
    others(i, lambda j: pl.semaphore_signal(barrier, inc=1, device_id={"dp": j}, device_id_type=MESH))
    others(t, lambda u: pl.semaphore_signal(barrier, inc=1, device_id={"tensor": u}, device_id_type=MESH))
    pl.semaphore_signal(barrier, inc=1, device_id={"group": 1 - g}, device_id_type=MESH)

    def hot(index):
        count = place_v.shape[1]
        equal = lax.broadcasted_iota(jnp.int32, (tokens, count), 0) == index
        return jnp.where(equal, 1.0, 0.0)

    back_v[...] = hot(send_ref[...]).astype(jnp.bfloat16)

    @pl.loop(0, rows_out.shape[0] // TILE)
    def _(k):
        rows_out[columns(k), :] = tn(back_v[:, columns(k)], source_ref[...]).astype(jnp.bfloat16)

    pl.semaphore_wait(barrier, 2 * (n - 1) + 1)

    others(i, lambda j: rows_to(j).start())

    def start_w(side, s, inside, onward):
        @pl.when(onward)
        def _():
            w_first(side).start()

    at_distance(0, start_w)
    rows_in[slot_rows(i), :] = rows_out[slot_rows(i), :]
    place = hot(recv_ref[...])
    place_v[...] = place.astype(jnp.bfloat16)
    paired = jnp.max(place, axis=1, keepdims=True)
    prompts = heads_ref.shape[0]
    length = tokens // prompts
    for p in range(prompts):
        rows = slice(p * length, (p + 1) * length)
        choose_v[rows, :] = (paired[rows, :] * heads_ref[p : p + 1, :]).astype(jnp.bfloat16)

    others(i, lambda j: rows_from(j).wait_recv())

    @pl.loop(0, width // TILE)
    def _(k):
        c = columns(k)
        incoming = nn(place_v[...], rows_in[:, c])
        chosen = choose_v[:, c].astype(jnp.float32) > 0.5
        mixed_all[i, :, c] = jnp.where(chosen, incoming, base_ref[:, c].astype(jnp.float32)).astype(jnp.bfloat16)
        grad_acc[:, c] = jnp.zeros((tokens, TILE), jnp.float32)

    def m_onward(side, inside):
        return inside & ((i + 1 < n) if side == 0 else (i >= 1))

    def start_m(side, s, inside, onward):
        @pl.when(m_onward(side, inside))
        def _():
            m_pass(side, s).start()

    for load in loads:
        load.wait()

    def blocks_taken(kind, body):
        others(i, lambda j: body(kind, j))

    def share_cot(kind, j):
        cot_in(kind, j, t).wait_recv()
        others(t, lambda u: cot_share(kind, j, u).start())

    def use_weight(s):
        @pl.loop(0, width // TILE)
        def _(k):
            c = columns(k)
            part_out[s, :, c] = nn(mixed_all[i], w_all[s, :, c]).astype(jnp.bfloat16)
            grad_acc[:, c] += nt(cot_own[s], w_all[s, c, :])

        @pl.when(s != t)
        def _():
            part_to(s).start()

    def use_tokens(j):
        others(t, lambda u: cot_in(0, j, u).wait_recv())

        @pl.loop(0, width // TILE)
        def _(k):
            c = columns(k)
            grad_weight_ref[c, :] += tn(mixed_all[j, :, c], cot_all[0, j])

    def m_used(side, s, inside, onward):
        @pl.when(inside)
        def _():
            use_tokens(s)

    def w_used(side, s, inside, onward):
        @pl.when(inside)
        def _():
            w_across_in(s).wait_recv()
            use_weight(s)

    def w_arrives(side, s, inside, onward):
        @pl.when(inside)
        def _():
            w_pass(side, s).wait_recv()

            @pl.when(onward)
            def _():
                w_pass(side, s).start()

            w_across(s).start()

    def m_arrives(side, s, inside, onward):
        @pl.when(inside)
        def _():
            m_pass(side, s).wait_recv()

            @pl.when(m_onward(side, inside))
            def _():
                m_pass(side, s).start()

    at_distance(1, w_arrives)
    at_distance(0, start_m)
    cot_sent(lambda copy: copy.start(), (0, n - 1))
    use_weight(i)
    at_distance(2, w_arrives)
    at_distance(1, m_arrives)
    cot_sent(lambda copy: copy.start(), range(1, n - 1))
    at_distance(1, w_used)
    at_distance(3, w_arrives)
    at_distance(2, w_used)
    at_distance(2, m_arrives)

    blocks_taken(0, share_cot)
    at_distance(3, w_used)

    others(i, lambda j: rows_to(j).wait_send())

    @pl.loop(0, width // TILE)
    def _(k):
        c = columns(k)
        chosen = choose_v[:, c].astype(jnp.float32) > 0.5
        grad = grad_acc[:, c]
        zero = jnp.zeros_like(grad)
        grad_base_ref[:, c] = jnp.where(chosen, zero, grad).astype(jnp.bfloat16)
        swapped_v[:, c] = jnp.where(chosen, grad, zero).astype(jnp.bfloat16)

    @pl.loop(0, rows_out.shape[0] // TILE)
    def _(k):
        rows_out[columns(k), :] = tn(place_v[:, columns(k)], swapped_v[...]).astype(jnp.bfloat16)

    others(i, lambda j: rows_home(j).start())
    home_ref[slot_rows(i), :] = rows_out[slot_rows(i), :]

    @pl.loop(0, width // TILE)
    def _(k):
        grad_weight_ref[columns(k), :] = tn(mixed_all[i, :, columns(k)], cot_own[i])

    at_distance(1, m_used)
    at_distance(2, m_used)
    at_distance(3, m_arrives)
    at_distance(3, m_used)

    others(t, lambda u: part_from(u).wait_recv())
    part_in[t] = part_out[t]

    @pl.loop(0, width // TILE)
    def _(k):
        c = columns(k)
        total = res_v[:, c].astype(jnp.float32)
        summed = part_in[0, :, c].astype(jnp.float32)
        for u in range(1, n):
            summed += part_in[u, :, c].astype(jnp.float32)
        layer_ref[:, c] = (summed + total).astype(jnp.bfloat16)

    others(i, lambda j: rows_home_in(j).wait_recv())

    @pl.loop(0, width // TILE)
    def _(k):
        c = columns(k)
        grad_source_ref[:, c] = nn(back_v[...], home_ref[:, c]).astype(jnp.bfloat16)

    cot_sent(lambda copy: copy.wait_send(), range(n))
    others(i, lambda j: rows_home(j).wait_send())
    others(t, lambda u: part_to(u).wait_send())
    for kind in range(1):
        blocks_taken(kind, lambda kind, j: others(t, lambda u: cot_share(kind, j, u).wait_send()))

    def drain(k, carry):
        def sent(side, s, inside, onward):
            @pl.when(onward)
            def _():
                w_pass(side, s).wait_send()

            @pl.when(m_onward(side, inside) & (k < n))
            def _():
                m_pass(side, s).wait_send()

            @pl.when(inside & (k >= 1))
            def _():
                w_across(s).wait_send()

        at_distance(k, sent)
        return carry

    lax.fori_loop(0, n, drain, 0)


def copy_out(*refs):
    for k in range(4):
        refs[4 + k][...] = refs[k][...]


def with_kernel(
    base_heads, source_heads, residual, weight, cotangent, send_slots, recv_slots, head_mask
):
    rows, width = base_heads.shape
    n = send_slots.shape[1]
    slots = n * send_slots.shape[2]
    depth, block = weight.shape
    prompts, heads_here = head_mask.shape
    heads = jnp.repeat(head_mask, width // heads_here, axis=1).astype(jnp.float32)
    kept = pl.BlockSpec(memory_space=pl.ANY)
    near = pl.BlockSpec(memory_space=pltpu.VMEM)
    dma = pltpu.SemaphoreType.DMA
    bf16 = jnp.bfloat16
    results = pl.pallas_call(
        functools.partial(fused, n),
        out_shape=(
            jax.ShapeDtypeStruct((rows, width), bf16),
            jax.ShapeDtypeStruct((rows, width), bf16),
            jax.ShapeDtypeStruct((rows, width), bf16),
            jax.ShapeDtypeStruct((depth, block), jnp.float32),
        ),
        in_specs=[kept] * 3 + [near] * 5,
        out_specs=(near,) * 4,
        scratch_shapes=[
            pltpu.VMEM((n, depth, block), bf16),
            pltpu.VMEM((n, rows, block), bf16),
            pltpu.VMEM((1, n, rows, block), bf16),
            pltpu.VMEM((n, rows, width), bf16),
            pltpu.VMEM((slots, width), bf16),
            pltpu.VMEM((slots, width), bf16),
            pltpu.VMEM((slots, width), bf16),
            pltpu.VMEM((n, rows, block), bf16),
            pltpu.VMEM((n, rows, block), bf16),
            pltpu.VMEM((rows, width), jnp.float32),
            pltpu.VMEM((rows, width), bf16),
            pltpu.VMEM((rows, width), bf16),
            pltpu.VMEM((rows, slots), bf16),
            pltpu.VMEM((rows, slots), bf16),
            pltpu.VMEM((rows, width), bf16),
            dma((n + 2,)),
            dma((2, n)),
            dma((n,)),
            dma((n,)),
            dma((n,)),
            dma((2, n)),
            dma((n,)),
            dma((n,)),
            dma((n,)),
            dma((n,)),
            dma((n,)),
            dma((n,)),
            dma((1, n, n)),
            dma((1, n, n)),
            dma((n,)),
            dma((n,)),
        ],
        compiler_params=pltpu.CompilerParams(
            collective_id=0, has_side_effects=True, vmem_limit_bytes=60 * 1024 * 1024
        ),
    )(
        weight,
        cotangent,
        residual,
        base_heads,
        source_heads,
        send_slots.reshape(1, slots),
        recv_slots.reshape(1, slots),
        heads,
    )
    steps = 4
    blocks = [pl.BlockSpec((x.shape[0] // steps, x.shape[1]), lambda k: (k, 0)) for x in results]
    return pl.pallas_call(
        copy_out,
        grid=(steps,),
        out_shape=tuple(jax.ShapeDtypeStruct(x.shape, x.dtype) for x in results),
        in_specs=blocks,
        out_specs=tuple(blocks),
        compiler_params=pltpu.CompilerParams(vmem_limit_bytes=60 * 1024 * 1024),
    )(*results)


def solution(mesh):
    square = mesh.shape["dp"] == mesh.shape["tensor"] == 4 and mesh.shape["group"] == 2
    return jax.shard_map(
        with_kernel if square else with_collectives,
        mesh=mesh,
        in_specs=(
            P(("group", "dp"), "tensor"),
            P(("group", "dp"), "tensor"),
            P(("group", "dp"), "tensor"),
            P("tensor", "dp"),
            P(("group", "dp"), None),
            P(("group", "dp"), None, None),
            P(("group", "dp"), None, None),
            P(("group", "dp"), "tensor"),
        ),
        out_specs=(
            P(("group", "dp"), "tensor"),
            P(("group", "dp"), "tensor"),
            P(("group", "dp"), "tensor"),
            P(("group", "tensor"), "dp"),
        ),
        check_vma=False,
    )
```

```python
import functools

import jax
import jax.numpy as jnp
from jax import lax
from jax.experimental import pallas as pl
from jax.experimental.pallas import tpu as pltpu
from jax.sharding import PartitionSpec as P


def with_collectives(
    base_heads, source_heads, residual, weight, cotangent, send_slots, recv_slots, head_mask
):
    rows, width = base_heads.shape
    peers = send_slots.shape[1]
    slots = send_slots.shape[2]
    prompts, heads_here = head_mask.shape
    head_size = width // heads_here
    prompt_len = rows // prompts
    send_index = send_slots.reshape(-1)
    send_live = send_index >= 0
    outgoing = jnp.where(
        send_live[:, None], source_heads[jnp.maximum(send_index, 0)], jnp.zeros((), jnp.bfloat16)
    )
    arrived = lax.all_to_all(
        outgoing.reshape(peers, slots, width), "dp", split_axis=0, concat_axis=0, tiled=True
    ).reshape(peers * slots, width)
    recv_index = recv_slots.reshape(-1)
    recv_live = recv_index >= 0
    target = jnp.where(recv_live, recv_index, rows)
    incoming = jnp.zeros((rows, width), jnp.bfloat16).at[target].set(arrived, mode="drop")
    paired = jnp.zeros((rows,), jnp.int32).at[target].set(1, mode="drop")
    mask_rows = jnp.repeat(jnp.repeat(head_mask, prompt_len, axis=0), head_size, axis=1)
    choose = (paired[:, None] == 1) & (mask_rows == 1)
    mixed = jnp.where(choose, incoming, base_heads)
    partial_sum = jnp.dot(
        mixed, lax.all_gather(weight, "dp", axis=1, tiled=True), preferred_element_type=jnp.float32
    )
    attn = lax.psum_scatter(
        partial_sum.astype(jnp.bfloat16), "tensor", scatter_dimension=1, tiled=True
    ).astype(jnp.float32)
    layer_out = (attn + residual.astype(jnp.float32)).astype(jnp.bfloat16)
    grad_wide = lax.dot_general(
        cotangent,
        lax.all_gather(weight, "dp", axis=1, tiled=True),
        (((1,), (1,)), ((), ())),
        preferred_element_type=jnp.float32,
    )
    grad_mixed = grad_wide.astype(jnp.bfloat16)
    zero = jnp.zeros((), jnp.bfloat16)
    grad_base = jnp.where(choose, zero, grad_mixed)
    back_rows = jnp.where(recv_live, recv_index, 0)
    returned = jnp.where(recv_live[:, None] & choose[back_rows], grad_mixed[back_rows], zero)
    homeward = lax.all_to_all(
        returned.reshape(peers, slots, width), "dp", split_axis=0, concat_axis=0, tiled=True
    ).reshape(peers * slots, width)
    source_target = jnp.where(send_live, send_index, rows)
    grad_source = (
        jnp.zeros((rows, width), jnp.bfloat16).at[source_target].add(homeward, mode="drop")
    )
    grad_term = lax.dot_general(
        mixed, cotangent, (((0,), (0,)), ((), ())), preferred_element_type=jnp.float32
    )
    grad_weight = lax.psum_scatter(
        grad_term.astype(jnp.bfloat16), "dp", scatter_dimension=1, tiled=True
    ).astype(jnp.float32)
    return (layer_out, grad_base, grad_source, grad_weight)


MESH = pl.DeviceIdType.MESH
TILE = 256


def nn(a, b):
    return jnp.dot(a, b, preferred_element_type=jnp.float32)


def nt(a, b):
    return lax.dot_general(a, b, (((1,), (1,)), ((), ())), preferred_element_type=jnp.float32)


def tn(a, b):
    return lax.dot_general(a, b, (((0,), (0,)), ((), ())), preferred_element_type=jnp.float32)


def fused(
    n,
    weight_ref,
    cotangent_ref,
    residual_ref,
    base_ref,
    source_ref,
    send_ref,
    recv_ref,
    heads_ref,
    layer_ref,
    grad_base_ref,
    grad_source_ref,
    grad_weight_ref,
    w_all,
    cot_own,
    cot_all,
    mixed_all,
    rows_out,
    rows_in,
    home_ref,
    part_out,
    part_in,
    grad_acc,
    res_v,
    choose_v,
    place_v,
    back_v,
    swapped_v,
    end_out,
    end_in,
    local_sem,
    w_send,
    w_recv,
    y_send,
    y_recv,
    m_send,
    m_recv,
    s_send,
    s_recv,
    h_send,
    h_recv,
    c_send,
    c_recv,
    b_send,
    p_send,
    p_recv,
    e_send,
    e_recv,
):
    g = lax.axis_index("group")
    i = lax.axis_index("dp")
    t = lax.axis_index("tensor")
    tokens, width = base_ref.shape
    half = w_all.shape[1] // 2
    block = w_all.shape[2]
    slots = rows_out.shape[0] // n
    quarter = tokens // n
    middle = (i >= 1) & (i <= n - 2)
    beside_end = (i == 1) | (i == n - 2)
    end = jnp.where(i <= 1, 0, n - 1)

    def remote(src, dst, send, recv, to):
        return pltpu.make_async_remote_copy(
            src_ref=src, dst_ref=dst, send_sem=send, recv_sem=recv, device_id=to, device_id_type=MESH
        )

    def columns(k):
        return pl.ds(pl.multiple_of(k * TILE, TILE), TILE)

    def mine():
        return pl.ds(pl.multiple_of(g * half, half), half)

    def theirs():
        return pl.ds(pl.multiple_of((1 - g) * half, half), half)

    def strip(k):
        return pl.ds(pl.multiple_of(k * quarter, quarter), quarter)

    def slot_rows(k):
        return pl.ds(pl.multiple_of(k * slots, slots), slots)

    def w_first(side):
        to = jnp.clip(i + 1 - 2 * side, 0, n - 1)
        return remote(
            weight_ref.at[mine(), :], w_all.at[i, mine(), :], w_send.at[side, i], w_recv.at[i], {"dp": to}
        )

    def w_pass(side, s):
        to = jnp.clip(i + 1 - 2 * side, 0, n - 1)
        return remote(
            w_all.at[s, mine(), :], w_all.at[s, mine(), :], w_send.at[side, s], w_recv.at[s], {"dp": to}
        )

    def w_across(s):
        return remote(
            w_all.at[s, mine(), :], w_all.at[s, mine(), :], y_send.at[s], y_recv.at[s], {"group": 1 - g}
        )

    def w_across_in(s):
        return remote(
            w_all.at[s, theirs(), :], w_all.at[s, theirs(), :], y_send.at[s], y_recv.at[s], {"group": 1 - g}
        )

    def m_pass(side, s):
        to = jnp.clip(i + 1 - 2 * side, 0, n - 1)
        return remote(mixed_all.at[s], mixed_all.at[s], m_send.at[side, s], m_recv.at[s], {"dp": to})

    def rows_to(j):
        return remote(rows_out.at[slot_rows(j), :], rows_in.at[slot_rows(i), :], s_send.at[j], s_recv.at[i], {"dp": j})

    def rows_from(j):
        return remote(rows_out.at[slot_rows(j), :], rows_in.at[slot_rows(j), :], s_send.at[j], s_recv.at[j], {"dp": j})

    def rows_home(j):
        return remote(rows_out.at[slot_rows(j), :], home_ref.at[slot_rows(i), :], h_send.at[j], h_recv.at[i], {"dp": j})

    def rows_home_in(j):
        return remote(rows_out.at[slot_rows(j), :], home_ref.at[slot_rows(j), :], h_send.at[j], h_recv.at[j], {"dp": j})

    def cot_to(b):
        kind = 0 if 0 < b < n - 1 else 1
        taker = min(max(b, 1), n - 2)
        return remote(
            cotangent_ref.at[strip(t), b * block : (b + 1) * block],
            cot_all.at[kind, i, strip(t), :],
            c_send.at[b],
            c_recv.at[kind, i, t],
            {"dp": taker},
        )

    def cot_sent(body, blocks):
        for b in blocks:
            taker = min(max(b, 1), n - 2)

            @pl.when((i != b) & (i != taker))
            def _():
                body(cot_to(b))

    def cot_share(kind, j, u):
        piece = cot_all.at[kind, j, strip(t), :]
        return remote(piece, piece, b_send.at[kind, j, u], c_recv.at[kind, j, t], {"tensor": u})

    def cot_in(kind, j, u):
        piece = cot_all.at[kind, j, strip(u), :]
        return remote(piece, piece, b_send.at[kind, j, u], c_recv.at[kind, j, u], {"tensor": u})

    def end_pass():
        return remote(end_out, end_in, e_send.at[0], e_recv.at[0], {"dp": end})

    def part_to(u):
        return remote(part_out.at[u], part_in.at[t], p_send.at[u], p_recv.at[t], {"tensor": u})

    def part_from(u):
        return remote(part_out.at[u], part_in.at[u], p_send.at[u], p_recv.at[u], {"tensor": u})

    def others(me, body):
        def step(k, carry):
            body(lax.rem(me + k, n))
            return carry

        lax.fori_loop(1, n, step, 0)

    def at_distance(k, body):
        for side in range(2):
            s = i - k if side == 0 else i + k
            inside = (s >= 0) & (s < n)
            onward = inside & ((i + 1 < n) if side == 0 else (i >= 1))
            body(side, jnp.clip(s, 0, n - 1), inside, onward)

    loads = [pltpu.make_async_copy(weight_ref, w_all.at[i], local_sem.at[0])]
    for k in range(n):
        loads.append(
            pltpu.make_async_copy(
                cotangent_ref.at[:, k * block : (k + 1) * block], cot_own.at[k], local_sem.at[1 + k]
            )
        )
    loads.append(pltpu.make_async_copy(residual_ref, res_v, local_sem.at[1 + n]))
    for load in loads:
        load.start()

    barrier = pltpu.get_barrier_semaphore()
    others(i, lambda j: pl.semaphore_signal(barrier, inc=1, device_id={"dp": j}, device_id_type=MESH))
    others(t, lambda u: pl.semaphore_signal(barrier, inc=1, device_id={"tensor": u}, device_id_type=MESH))
    pl.semaphore_signal(barrier, inc=1, device_id={"group": 1 - g}, device_id_type=MESH)

    def hot(index):
        count = place_v.shape[1]
        equal = lax.broadcasted_iota(jnp.int32, (tokens, count), 0) == index
        return jnp.where(equal, 1.0, 0.0)

    back_v[...] = hot(send_ref[...]).astype(jnp.bfloat16)

    @pl.loop(0, rows_out.shape[0] // TILE)
    def _(k):
        rows_out[columns(k), :] = tn(back_v[:, columns(k)], source_ref[...]).astype(jnp.bfloat16)

    pl.semaphore_wait(barrier, 2 * (n - 1) + 1)

    others(i, lambda j: rows_to(j).start())

    def start_w(side, s, inside, onward):
        @pl.when(onward)
        def _():
            w_first(side).start()

    at_distance(0, start_w)
    rows_in[slot_rows(i), :] = rows_out[slot_rows(i), :]
    place = hot(recv_ref[...])
    place_v[...] = place.astype(jnp.bfloat16)
    paired = jnp.max(place, axis=1, keepdims=True)
    prompts = heads_ref.shape[0]
    length = tokens // prompts
    for p in range(prompts):
        rows = slice(p * length, (p + 1) * length)
        choose_v[rows, :] = (paired[rows, :] * heads_ref[p : p + 1, :]).astype(jnp.bfloat16)

    others(i, lambda j: rows_from(j).wait_recv())

    @pl.loop(0, width // TILE)
    def _(k):
        c = columns(k)
        incoming = nn(place_v[...], rows_in[:, c])
        chosen = choose_v[:, c].astype(jnp.float32) > 0.5
        mixed_all[i, :, c] = jnp.where(chosen, incoming, base_ref[:, c].astype(jnp.float32)).astype(jnp.bfloat16)
        grad_acc[:, c] = jnp.zeros((tokens, TILE), jnp.float32)

    def m_onward(side, inside):
        return inside & ((i + 1 <= n - 2) if side == 0 else (i - 1 >= 1))

    def start_m(side, s, inside, onward):
        @pl.when(m_onward(side, inside))
        def _():
            m_pass(side, s).start()

    for load in loads:
        load.wait()

    def blocks_taken(kind, body):
        @pl.when(middle if kind == 0 else beside_end)
        def _():
            def one(j):
                if kind == 0:
                    body(kind, j)
                else:

                    @pl.when(j != end)
                    def _():
                        body(kind, j)

            others(i, one)

    def share_cot(kind, j):
        cot_in(kind, j, t).wait_recv()
        others(t, lambda u: cot_share(kind, j, u).start())

    def use_weight(s):
        @pl.loop(0, width // TILE)
        def _(k):
            c = columns(k)
            part_out[s, :, c] = nn(mixed_all[i], w_all[s, :, c]).astype(jnp.bfloat16)
            grad_acc[:, c] += nt(cot_own[s], w_all[s, c, :])

        @pl.when(s != t)
        def _():
            part_to(s).start()

    def use_tokens(j):
        others(t, lambda u: cot_in(0, j, u).wait_recv())

        @pl.loop(0, width // TILE)
        def _(k):
            c = columns(k)
            grad_weight_ref[c, :] += tn(mixed_all[j, :, c], cot_all[0, j])

    def end_terms():
        blocks_taken(1, lambda kind, j: others(t, lambda u: cot_in(kind, j, u).wait_recv()))
        first = lax.rem(end + 1, n)
        second = lax.rem(end + 2, n)
        third = lax.rem(end + 3, n)
        cot_all[1, i] = cot_own[end]

        @pl.loop(0, width // TILE)
        def _(k):
            c = columns(k)
            total = tn(mixed_all[first, :, c], cot_all[1, first])
            total += tn(mixed_all[second, :, c], cot_all[1, second])
            total += tn(mixed_all[third, :, c], cot_all[1, third])
            end_out[c, :] = total.astype(jnp.bfloat16)

        end_pass().start()

    def w_used(side, s, inside, onward):
        @pl.when(inside)
        def _():
            w_across_in(s).wait_recv()
            use_weight(s)

    def w_arrives(side, s, inside, onward):
        @pl.when(inside)
        def _():
            w_pass(side, s).wait_recv()

            @pl.when(onward)
            def _():
                w_pass(side, s).start()

            w_across(s).start()

    def m_arrives(side, s, inside, onward):
        @pl.when(inside & middle)
        def _():
            m_pass(side, s).wait_recv()

            @pl.when(m_onward(side, inside))
            def _():
                m_pass(side, s).start()

    at_distance(1, w_arrives)
    at_distance(0, start_m)
    cot_sent(lambda copy: copy.start(), (0, n - 1))
    use_weight(i)

    @pl.loop(0, width // TILE)
    def _(k):
        grad_weight_ref[columns(k), :] = tn(mixed_all[i, :, columns(k)], cot_own[i])

    at_distance(2, w_arrives)
    at_distance(1, m_arrives)
    cot_sent(lambda copy: copy.start(), range(1, n - 1))
    at_distance(1, w_used)
    blocks_taken(1, share_cot)
    at_distance(3, w_arrives)
    at_distance(2, w_used)
    blocks_taken(0, share_cot)
    at_distance(2, m_arrives)

    @pl.when(beside_end)
    def _():
        end_terms()

    at_distance(3, w_used)

    others(i, lambda j: rows_to(j).wait_send())

    @pl.loop(0, width // TILE)
    def _(k):
        c = columns(k)
        chosen = choose_v[:, c].astype(jnp.float32) > 0.5
        grad = grad_acc[:, c]
        zero = jnp.zeros_like(grad)
        grad_base_ref[:, c] = jnp.where(chosen, zero, grad).astype(jnp.bfloat16)
        swapped_v[:, c] = jnp.where(chosen, grad, zero).astype(jnp.bfloat16)

    @pl.loop(0, rows_out.shape[0] // TILE)
    def _(k):
        rows_out[columns(k), :] = tn(place_v[:, columns(k)], swapped_v[...]).astype(jnp.bfloat16)

    others(i, lambda j: rows_home(j).start())
    home_ref[slot_rows(i), :] = rows_out[slot_rows(i), :]

    @pl.when(middle)
    def _():
        others(i, use_tokens)

    others(t, lambda u: part_from(u).wait_recv())
    part_in[t] = part_out[t]

    @pl.loop(0, width // TILE)
    def _(k):
        c = columns(k)
        total = res_v[:, c].astype(jnp.float32)
        summed = part_in[0, :, c].astype(jnp.float32)
        for u in range(1, n):
            summed += part_in[u, :, c].astype(jnp.float32)
        layer_ref[:, c] = (summed + total).astype(jnp.bfloat16)

    others(i, lambda j: rows_home_in(j).wait_recv())

    @pl.loop(0, width // TILE)
    def _(k):
        c = columns(k)
        grad_source_ref[:, c] = nn(back_v[...], home_ref[:, c]).astype(jnp.bfloat16)

    @pl.when(jnp.logical_not(middle))
    def _():
        end_pass().wait_recv()

        @pl.loop(0, width // TILE)
        def _(k):
            grad_weight_ref[columns(k), :] += end_in[columns(k), :].astype(jnp.float32)

    @pl.when(beside_end)
    def _():
        end_pass().wait_send()

    cot_sent(lambda copy: copy.wait_send(), range(n))
    others(i, lambda j: rows_home(j).wait_send())
    others(t, lambda u: part_to(u).wait_send())
    for kind in range(2):
        blocks_taken(kind, lambda kind, j: others(t, lambda u: cot_share(kind, j, u).wait_send()))

    def drain(k, carry):
        def sent(side, s, inside, onward):
            @pl.when(onward)
            def _():
                w_pass(side, s).wait_send()

            @pl.when(m_onward(side, inside) & (middle | (k == 0)))
            def _():
                m_pass(side, s).wait_send()

            @pl.when(inside & (k >= 1))
            def _():
                w_across(s).wait_send()

        at_distance(k, sent)
        return carry

    lax.fori_loop(0, n, drain, 0)


def copy_out(*refs):
    for k in range(4):
        refs[4 + k][...] = refs[k][...]


def with_kernel(
    base_heads, source_heads, residual, weight, cotangent, send_slots, recv_slots, head_mask
):
    rows, width = base_heads.shape
    n = send_slots.shape[1]
    slots = n * send_slots.shape[2]
    depth, block = weight.shape
    prompts, heads_here = head_mask.shape
    heads = jnp.repeat(head_mask, width // heads_here, axis=1).astype(jnp.float32)
    kept = pl.BlockSpec(memory_space=pl.ANY)
    near = pl.BlockSpec(memory_space=pltpu.VMEM)
    dma = pltpu.SemaphoreType.DMA
    bf16 = jnp.bfloat16
    results = pl.pallas_call(
        functools.partial(fused, n),
        out_shape=(
            jax.ShapeDtypeStruct((rows, width), bf16),
            jax.ShapeDtypeStruct((rows, width), bf16),
            jax.ShapeDtypeStruct((rows, width), bf16),
            jax.ShapeDtypeStruct((depth, block), jnp.float32),
        ),
        in_specs=[kept] * 3 + [near] * 5,
        out_specs=(near,) * 4,
        scratch_shapes=[
            pltpu.VMEM((n, depth, block), bf16),
            pltpu.VMEM((n, rows, block), bf16),
            pltpu.VMEM((2, n, rows, block), bf16),
            pltpu.VMEM((n, rows, width), bf16),
            pltpu.VMEM((slots, width), bf16),
            pltpu.VMEM((slots, width), bf16),
            pltpu.VMEM((slots, width), bf16),
            pltpu.VMEM((n, rows, block), bf16),
            pltpu.VMEM((n, rows, block), bf16),
            pltpu.VMEM((rows, width), jnp.float32),
            pltpu.VMEM((rows, width), bf16),
            pltpu.VMEM((rows, width), bf16),
            pltpu.VMEM((rows, slots), bf16),
            pltpu.VMEM((rows, slots), bf16),
            pltpu.VMEM((rows, width), bf16),
            pltpu.VMEM((depth, block), bf16),
            pltpu.VMEM((depth, block), bf16),
            dma((n + 2,)),
            dma((2, n)),
            dma((n,)),
            dma((n,)),
            dma((n,)),
            dma((2, n)),
            dma((n,)),
            dma((n,)),
            dma((n,)),
            dma((n,)),
            dma((n,)),
            dma((n,)),
            dma((2, n, n)),
            dma((2, n, n)),
            dma((n,)),
            dma((n,)),
            dma((1,)),
            dma((1,)),
        ],
        compiler_params=pltpu.CompilerParams(
            collective_id=0, has_side_effects=True, vmem_limit_bytes=60 * 1024 * 1024
        ),
    )(
        weight,
        cotangent,
        residual,
        base_heads,
        source_heads,
        send_slots.reshape(1, slots),
        recv_slots.reshape(1, slots),
        heads,
    )
    steps = 8
    blocks = [pl.BlockSpec((x.shape[0] // steps, x.shape[1]), lambda k: (k, 0)) for x in results]
    return pl.pallas_call(
        copy_out,
        grid=(steps,),
        out_shape=tuple(jax.ShapeDtypeStruct(x.shape, x.dtype) for x in results),
        in_specs=blocks,
        out_specs=tuple(blocks),
        compiler_params=pltpu.CompilerParams(vmem_limit_bytes=60 * 1024 * 1024),
    )(*results)


def solution(mesh):
    square = mesh.shape["dp"] == mesh.shape["tensor"] == 4 and mesh.shape["group"] == 2
    return jax.shard_map(
        with_kernel if square else with_collectives,
        mesh=mesh,
        in_specs=(
            P(("group", "dp"), "tensor"),
            P(("group", "dp"), "tensor"),
            P(("group", "dp"), "tensor"),
            P("tensor", "dp"),
            P(("group", "dp"), None),
            P(("group", "dp"), None, None),
            P(("group", "dp"), None, None),
            P(("group", "dp"), "tensor"),
        ),
        out_specs=(
            P(("group", "dp"), "tensor"),
            P(("group", "dp"), "tensor"),
            P(("group", "dp"), "tensor"),
            P(("group", "tensor"), "dp"),
        ),
        check_vma=False,
    )
```
